32 devices in a mesh: pairs: 8 (over z, x), tm: 4 (over y, core).
Axes of the slice: x: 2, y: 2, z: 4, core: 2. Of those that a mesh axis runs over, the one named last changes fastest.
Arguments:
- traces: float32 [8, 512, 6144], P('tm', 'pairs'), may hold values from -64 to 64
- station_slot: int32 [512], replicated, may hold values from 0 to 511, as said below
- pair_stations: int32 [512, 2], P('pairs'), may hold values from 0 to 511, as said below
Outputs:
- correlation_stack: float32 [2048, 512], P('tm', 'pairs')
The draws below stay inside these ranges and needn't reach their ends.
Inputs may be any that keep to these rules, and one draw needn't show every extreme that they name: `station_slot`: A permutation: rows r * 64 to (r + 1) * 64 - 1 of traces are the stations of owner r. `pair_stations`: in each block of 64 pairs (the pairs of one device), at most 32 of the 128 pair ends name stations whose station_slot // 64 is one value, and in every block one value is named by exactly 32 ends. A pair may name one station twice.
All inputs are finite; a program needn't handle non-finite values.
Results may differ from the reference program's by a relative error of at most 0.011.
Values may be sent and summed in bfloat16 or wider, within the bound.
A program may use at most 64 MiB of HBM per device.

```python
import math
import jax
import jax.numpy as jnp
from jax import lax

NS = 6144
F = 1536
FLO = 32
LAG = 1024
S_DEV = 64
P_DEV = 64
STATIONS = 512
WINDOWS = 8
CAP = 32


def slot_order(key):
    return jax.random.permutation(jax.random.fold_in(key, 11), STATIONS).astype(jnp.int32)


def draw_station_slot(key, part):
    return slot_order(key)


def draw_pair_stations(key, part):
    permuted = slot_order(key)
    slot_station = jnp.zeros((STATIONS,), jnp.int32).at[permuted].set(jnp.arange(STATIONS, dtype=jnp.int32))
    blocks = STATIONS // S_DEV
    end_total = 2 * P_DEV
    draw_key = jax.random.fold_in(key, 23)
    busiest = jax.random.randint(jax.random.fold_in(draw_key, 1), (blocks,), 0, blocks)

    def one_block(block_index):
        block_key = jax.random.fold_in(draw_key, 100 + block_index)
        picked = jax.random.permutation(jax.random.fold_in(block_key, 1), (blocks - 1) * CAP)[:end_total - CAP]
        others = (picked // CAP).astype(jnp.int32)
        others = others + (others >= busiest[block_index]).astype(jnp.int32)
        owners = jnp.concatenate([jnp.full((CAP,), busiest[block_index], jnp.int32), others])
        owners = jax.random.permutation(jax.random.fold_in(block_key, 2), owners)
        local_rows = jax.random.randint(jax.random.fold_in(block_key, 3), (end_total,), 0, S_DEV)
        return owners * S_DEV + local_rows
    slot_ids = jax.vmap(one_block)(jnp.arange(blocks, dtype=jnp.int32))
    return slot_station[slot_ids.reshape(blocks * P_DEV, 2)]


def draw_traces(key, part):
    full_shape = (WINDOWS, STATIONS, NS)
    amplitude = jnp.exp(jax.random.uniform(jax.random.fold_in(key, 5), (1, STATIONS, 1), minval=0.0, maxval=math.log(10.0)))
    samples = jnp.clip(jax.random.normal(jax.random.fold_in(key, 6), full_shape), -6.0, 6.0)
    return (samples * amplitude).astype(jnp.float32)


def setup_inputs(seed: int = 0) -> dict:
    streams_of = jax.random.split(jax.random.key(seed), 4)
    return {
        "traces": draw_traces(jax.random.fold_in(streams_of[3], 71), 0),
        "station_slot": draw_station_slot(jax.random.fold_in(streams_of[3], 71), 0),
        "pair_stations": draw_pair_stations(jax.random.fold_in(streams_of[3], 71), 0),
    }


two_pi = 6.283185307179586

def tapered_rows(traces):
    length = traces.shape[-1]
    sample_times = lax.iota(jnp.int32, length).astype(jnp.float32)
    hann_window = 0.5 - 0.5 * jnp.cos((sample_times + 0.5) * (two_pi / length))
    centred = traces - lax.optimization_barrier(jnp.mean(traces, axis=-1, keepdims=True))
    return (centred * hann_window).astype(jnp.bfloat16)

def forward_table(first_row, row_count, length, first_bin, bins):
    sample_times = first_row + lax.iota(jnp.int32, row_count)
    frequencies = first_bin + lax.iota(jnp.int32, bins)
    phases = sample_times[:, None] * frequencies[None, :] % length
    angles = phases.astype(jnp.float32) * (two_pi / length)
    return jnp.concatenate([jnp.cos(angles), -jnp.sin(angles)], axis=1).astype(jnp.bfloat16)

def whiten(spectrum, bins):
    real_part = spectrum[..., :bins]
    imag_part = spectrum[..., bins:]
    energy = real_part * real_part + imag_part * imag_part
    water_level = lax.optimization_barrier(jnp.mean(energy, axis=-1, keepdims=True))
    scaling = lax.rsqrt(energy + 0.1 * water_level + 1e-06)
    return jnp.concatenate([real_part * scaling, imag_part * scaling], axis=-1).astype(jnp.bfloat16)

def cross_spectra(left_ends, right_ends, bins):
    left_real = left_ends[..., :bins].astype(jnp.float32)
    left_imag = left_ends[..., bins:].astype(jnp.float32)
    right_real = right_ends[..., :bins].astype(jnp.float32)
    right_imag = right_ends[..., bins:].astype(jnp.float32)
    return jnp.concatenate([left_real * right_real + left_imag * right_imag, left_imag * right_real - left_real * right_imag], axis=-1)

def lag_block(stacked, first_row, row_count, first_bin, bins, length, half_span):
    lag_values = first_row + lax.iota(jnp.int32, row_count) - half_span
    frequencies = first_bin + lax.iota(jnp.int32, bins)
    phases = lag_values[:, None] * frequencies[None, :] % length
    angles = phases.astype(jnp.float32) * (two_pi / length)
    lag_table = jnp.concatenate([jnp.cos(angles), -jnp.sin(angles)], axis=1)
    return lax.dot_general(lag_table, stacked, (((1,), (1,)), ((), ())), precision=lax.Precision.HIGHEST, preferred_element_type=jnp.float32)

def reference(traces, station_slot, pair_stations):
    length = traces.shape[2]
    left_slots = station_slot[pair_stations[:, 0]]
    right_slots = station_slot[pair_stations[:, 1]]
    full_table = forward_table(0, length, length, FLO, F)

    def one_window(running, window):
        tapered = tapered_rows(window)
        spectrum = jnp.dot(tapered, full_table, preferred_element_type=jnp.float32)
        whitened = whiten(spectrum, F)
        return (running + cross_spectra(whitened[left_slots], whitened[right_slots], F), None)
    stacked, unused = lax.scan(one_window, jnp.zeros((pair_stations.shape[0], 2 * F), jnp.float32), traces)
    normalizer = 1.0 / math.sqrt(F * traces.shape[0])
    return lag_block(stacked, 0, 2 * LAG, FLO, F, length, LAG) * normalizer
```

```python
import functools
import math

import jax
import jax.numpy as jnp
import ml_dtypes
import numpy as np
from jax import lax
from jax.experimental import pallas as pl
from jax.experimental.pallas import tpu as pltpu
from jax.sharding import PartitionSpec as P

F = 1536
FLO = 32
LAG = 1024
RADIX = 8
MESH = pl.DeviceIdType.MESH
F32 = jnp.float32
BF16 = jnp.bfloat16


def share_bins(bins_each, tm):
    bins = bins_each // tm
    return bins, -(-bins // 16) * 16


def tables(length, blocks, tm):
    bins_each = F // blocks
    group = blocks // RADIX
    short = length // RADIX
    angles = 2.0 * np.pi * np.arange(length) / length
    cos_of = np.cos(angles).astype(np.float32).astype(ml_dtypes.bfloat16)
    sin_of = np.sin(angles).astype(np.float32).astype(ml_dtypes.bfloat16)
    block_ids = np.arange(blocks)
    first = block_ids // group + RADIX * (block_ids % group) * bins_each
    freqs = FLO + first[:, None] + RADIX * np.arange(bins_each)[None, :]
    phases = freqs[:, :, None] * np.arange(short)[None, None, :] % length
    forward = np.concatenate([cos_of[phases], sin_of[phases]], axis=1)

    bins, half = share_bins(bins_each, tm)
    inside = np.arange(half)
    value = np.arange(tm)[:, None] * bins + np.minimum(inside, bins - 1)[None, :]
    freq = freqs[block_ids[None, :, None], value[:, None, :]].reshape(-1)
    valid = np.broadcast_to(inside < bins, (tm, blocks, half)).reshape(-1)
    lag_phase = freq[None, :] * np.arange(2 * LAG // tm)[:, None] % length
    lag = np.stack([cos_of[lag_phase], -sin_of[lag_phase]])
    lag = np.where(valid, lag, np.zeros((), ml_dtypes.bfloat16))
    return forward.astype(ml_dtypes.bfloat16), lag.astype(ml_dtypes.bfloat16)


def kernel(
    blocks, tm, scale,
    x_hbm, hann, slot_col, ends, tab_hbm, lag_hbm, out,
    x, tab, lag, folded, water, spec_out, spec_in, water_in, ends_in, onehot, white,
    part_out, part_in, pack_out, pack_in, turn,
    local_sem, tab_sem, ends_s, ends_r, spec_s, spec_r, water_s, water_r,
    part_s, part_r, pack_s, pack_r, last_s, last_r,
):
    me, mine = lax.axis_index("pairs"), lax.axis_index("tm")
    bins_each = F // blocks
    group = blocks // RADIX
    length = x.shape[1]
    short = length // RADIX
    bins, half = share_bins(bins_each, tm)
    stations = onehot.shape[1]

    x_copy = pltpu.make_async_copy(x_hbm, x, local_sem.at[0])
    lag_copy = pltpu.make_async_copy(lag_hbm, lag, local_sem.at[1])
    x_copy.start()

    def step_of(i):
        return 1 + (i + blocks // 2 - 1) % (blocks - 1)

    def table_copy(s):
        return pltpu.make_async_copy(tab_hbm.at[(me + s) % blocks], tab.at[s], tab_sem.at[s])

    def start_table(i, c):
        table_copy(step_of(i)).start()
        return c

    lax.fori_loop(0, blocks - 1, start_table, 0)
    table_copy(0).start()
    lag_copy.start()

    def on_pairs(device):
        return {"pairs": device}

    def on_tm(device):
        return {"tm": device}

    barrier = pltpu.get_barrier_semaphore()
    for s in range(1, blocks):
        pl.semaphore_signal(barrier, inc=1, device_id=on_pairs((me + s) % blocks), device_id_type=MESH)
    for s in range(1, tm):
        pl.semaphore_signal(barrier, inc=1, device_id=on_tm((mine + s) % tm), device_id_type=MESH)
    pl.semaphore_wait(barrier, blocks + tm - 2)

    def remote(src, dst, send, recv, device):
        return pltpu.make_async_remote_copy(
            src_ref=src, dst_ref=dst, send_sem=send, recv_sem=recv, device_id=device, device_id_type=MESH
        )

    def ends_copy(s):
        return remote(ends, ends_in.at[me], ends_s.at[s], ends_r.at[s], on_pairs((me + s) % blocks))

    def spec_copy(s):
        return remote(spec_out.at[s], spec_in.at[me], spec_s.at[s], spec_r.at[s], on_pairs((me + s) % blocks))

    def water_copy(s):
        return remote(water, water_in.at[me], water_s.at[s], water_r.at[s], on_pairs((me + s) % blocks))

    def part_copy(s):
        to = (mine + s) % tm
        return remote(part_out.at[to], part_in.at[mine], part_s.at[s], part_r.at[s], on_tm(to))

    def pack_copy(s):
        to = (me + s) % blocks
        return remote(pack_out.at[to], pack_in.at[mine, me], pack_s.at[s], pack_r.at[s], on_pairs(to))

    def last_copy(s):
        return remote(pack_in.at[mine], pack_in.at[mine], last_s.at[s], last_r.at[s], on_tm((mine + s) % tm))

    def each(low, high, act):
        def body(s, c):
            act(s)
            return c
        lax.fori_loop(low, high, body, 0)

    each(1, blocks, lambda s: ends_copy(s).start())
    ends_in[me] = ends[...]

    x_copy.wait()
    root = math.sqrt(0.5)

    def fold(i, c):
        low = pl.ds(pl.multiple_of(i * 16, 16), 16)
        high = pl.ds(pl.multiple_of(128 + i * 16, 16), 16)
        mean = jnp.sum(x[low, :], axis=1, keepdims=True) * (1.0 / length)
        for k in range(short // 128):
            v = []
            for q in range(RADIX):
                cols = slice(q * short + k * 128, q * short + (k + 1) * 128)
                v.append((x[low, cols] - mean) * hann[0:1, cols])
            u = [v[q] + v[q + 4] for q in range(4)]
            d = [v[q] - v[q + 4] for q in range(4)]
            dm, dp = root * (d[1] - d[3]), root * (d[1] + d[3])
            even, odd = u[0] + u[2], u[1] + u[3]
            a2, b2 = u[0] - u[2], u[3] - u[1]
            a1, b1 = d[0] + dm, -d[2] - dp
            a3, b3 = d[0] - dm, d[2] - dp
            zero = jnp.zeros_like(even)
            classes = [
                (even + odd, zero), (a1, b1), (a2, b2), (a3, b3),
                (even - odd, zero), (a3, -b3), (a2, -b2), (a1, -b1),
            ]
            cols = slice(k * 128, (k + 1) * 128)
            for r, (a, b) in enumerate(classes):
                folded[r, low, cols] = a.astype(BF16)
                folded[r, high, cols] = b.astype(BF16)
        return c

    lax.fori_loop(0, 8, fold, 0)
    water[...] = jnp.zeros_like(water)

    def spectrum(s):
        table_copy(s).wait()
        to = (me + s) % blocks
        product = lax.dot_general(
            tab[s], folded[to // group], (((1,), (1,)), ((), ())), preferred_element_type=F32
        )
        re = product[:bins_each, :128] + product[bins_each:, 128:]
        im = product[:bins_each, 128:] - product[bins_each:, :128]
        water[...] += jnp.broadcast_to(jnp.sum(re * re + im * im, axis=0, keepdims=True), water.shape)
        return re.astype(BF16), im.astype(BF16)

    def send_block(i, c):
        s = step_of(i)
        re, im = spectrum(s)
        spec_out[s, :bins_each] = re
        spec_out[s, bins_each:] = im
        spec_copy(s).start()
        return c

    lax.fori_loop(0, blocks - 1, send_block, 0)
    re, im = spectrum(0)
    spec_in[me, :bins_each] = re
    spec_in[me, bins_each:] = im
    water_in[me] = water[...]
    each(1, blocks, lambda s: water_copy(s).start())

    lane = lax.broadcasted_iota(jnp.int32, (1, 128), 1)
    row_ids = lax.broadcasted_iota(jnp.int32, (stations, 256), 0).astype(F32)
    each(1, blocks, lambda s: ends_copy(s).wait())

    def swap(v):
        return pltpu.roll(v, 64, 1)

    def pick(g, c):
        a, b = ends_in[2 * g], ends_in[2 * g + 1]
        left = jnp.where(lane < 64, a, swap(b))[0:1]
        right = jnp.where(lane < 64, swap(a), b)[0:1]
        names = jnp.concatenate([left, right], axis=1)
        slots = jnp.sum(jnp.where(row_ids == names, slot_col[...], 0.0), axis=0, keepdims=True)
        onehot[g] = jnp.where(row_ids == slots, 1.0, 0.0).astype(BF16)
        return c

    lax.fori_loop(0, blocks // 2, pick, 0)

    first_lag = mine * (2 * LAG // tm) - LAG
    inner = lax.broadcasted_iota(jnp.int32, (half, 128), 0).astype(F32)

    def phase_turn(i, c):
        t, block = i // blocks, i % blocks
        base = FLO + block // group + RADIX * ((block % group) * bins_each + t * bins)
        product = (base.astype(F32) + RADIX * inner) * first_lag.astype(F32)
        phase = product - jnp.floor(product * (1.0 / length)) * length
        angle = phase * (2.0 * math.pi / length)
        sine = jnp.sin(angle)
        at = pl.ds(pl.multiple_of(i * half, half), half)
        turn[0, at, :] = jnp.cos(angle)
        turn[1, at, :] = jnp.where(lane < 64, -sine, sine)
        return c

    lax.fori_loop(0, tm * blocks, phase_turn, 0)

    each(1, blocks, lambda s: spec_copy(s).wait())
    each(1, blocks, lambda s: water_copy(s).wait())

    def whiten(src):
        re = spec_in[src, :bins_each].astype(F32)
        im = spec_in[src, bins_each:].astype(F32)
        level = water_in[src][0:1] * (0.1 / F) + 1e-6
        factor = lax.rsqrt(re * re + im * im + level)
        return re * factor, im * factor

    def whiten_two(q, c):
        cols = pl.ds(pl.multiple_of(q * 128, 128), 128)
        one, two = whiten(2 * q), whiten(2 * q + 1)
        for part in range(2):
            first = jnp.where(lane < 64, one[part], swap(two[part]))
            second = jnp.where(lane < 64, swap(one[part]), two[part])
            at = part * bins_each
            white[at:at + bins_each, cols] = first.astype(BF16)
            at += 2 * bins_each
            white[at:at + bins_each, cols] = second.astype(BF16)
        return c

    lax.fori_loop(0, blocks // 2, whiten_two, 0)

    if half > bins:
        part_out[...] = jnp.zeros_like(part_out)

    def cross(g, c):
        got = jnp.dot(white[...], onehot[g], preferred_element_type=F32)
        real = imag = None
        for w in range(2):
            at = 2 * w * bins_each
            lr, rr = got[at:at + bins_each, :128], got[at:at + bins_each, 128:]
            at += bins_each
            li, ri = got[at:at + bins_each, :128], got[at:at + bins_each, 128:]
            re, im = lr * rr + li * ri, li * rr - lr * ri
            real = re if real is None else real + re
            imag = im if imag is None else imag + im
        for t in range(tm):
            part_out[t, g, :bins] = real[t * bins:(t + 1) * bins].astype(BF16)
            part_out[t, g, half:half + bins] = imag[t * bins:(t + 1) * bins].astype(BF16)
        return c

    lax.fori_loop(0, blocks // 2, cross, 0)

    each(1, tm, lambda s: part_copy(s).start())
    part_in[mine] = part_out[mine]
    each(1, tm, lambda s: part_copy(s).wait())

    def pack(g, c):
        total = part_in[0, g].astype(F32)
        for t in range(1, tm):
            total += part_in[t, g].astype(F32)
        top, bottom = total[:half], total[half:]
        pack_out[2 * g] = jnp.where(lane < 64, top, swap(bottom)).astype(BF16)
        pack_out[2 * g + 1] = jnp.where(lane < 64, swap(top), bottom).astype(BF16)
        return c

    lax.fori_loop(0, blocks // 2, pack, 0)
    each(1, blocks, lambda s: pack_copy(s).start())
    pack_in[mine, me] = pack_out[me]
    each(1, blocks, lambda s: pack_copy(s).wait())
    each(1, tm, lambda s: last_copy(s).start())
    lag_copy.wait()
    each(1, tm, lambda s: last_copy(s).wait())

    stacked = pack_in[...].reshape(tm * blocks * half, 128).astype(F32)
    values = (stacked * turn[0] + swap(stacked) * turn[1]).astype(BF16)
    upper = jnp.dot(lag[0], values, preferred_element_type=F32)
    lower = jnp.dot(lag[1], values, preferred_element_type=F32)
    out[...] = ((upper + swap(lower)) * scale)[:, :64]


def on_device(traces, station_slot, pair_stations):
    held, stations_each, length = traces.shape
    stations = station_slot.shape[0]
    blocks, tm = lax.axis_size("pairs"), lax.axis_size("tm")
    pairs_each = pair_stations.shape[0]
    assert held * stations_each == 128 and held == 2 and pairs_each == 64 and blocks % RADIX == 0
    bins_each = F // blocks
    short = length // RADIX
    bins, half = share_bins(bins_each, tm)
    lag_rows = 2 * LAG // tm
    forward, lag = tables(length, blocks, tm)
    times = (np.arange(length, dtype=np.float64) + 0.5) * (2.0 * np.pi / length)
    hann = np.broadcast_to((0.5 - 0.5 * np.cos(times)).astype(np.float32), (8, length))
    ends = jnp.broadcast_to(pair_stations.T.reshape(1, 128).astype(F32), (8, 128))
    slot_col = station_slot.astype(F32).reshape(stations, 1)
    scale = 1.0 / math.sqrt(F * held * tm)
    vmem = pl.BlockSpec(memory_space=pltpu.VMEM)
    anywhere = pl.BlockSpec(memory_space=pl.ANY)
    dma = pltpu.SemaphoreType.DMA
    return pl.pallas_call(
        functools.partial(kernel, blocks, tm, scale),
        out_shape=jax.ShapeDtypeStruct((lag_rows, pairs_each), F32),
        in_specs=[anywhere, vmem, vmem, vmem, anywhere, anywhere],
        out_specs=vmem,
        scratch_shapes=[
            pltpu.VMEM((128, length), F32),
            pltpu.VMEM((blocks, 2 * bins_each, short), BF16),
            pltpu.VMEM((2, lag_rows, tm * blocks * half), BF16),
            pltpu.VMEM((RADIX, 256, short), BF16),
            pltpu.VMEM((8, 128), F32),
            pltpu.VMEM((blocks, 2 * bins_each, 128), BF16),
            pltpu.VMEM((blocks, 2 * bins_each, 128), BF16),
            pltpu.VMEM((blocks, 8, 128), F32),
            pltpu.VMEM((blocks, 8, 128), F32),
            pltpu.VMEM((blocks // 2, stations, 256), BF16),
            pltpu.VMEM((4 * bins_each, stations), BF16),
            pltpu.VMEM((tm, blocks // 2, 2 * half, 128), BF16),
            pltpu.VMEM((tm, blocks // 2, 2 * half, 128), BF16),
            pltpu.VMEM((blocks, half, 128), BF16),
            pltpu.VMEM((tm, blocks, half, 128), BF16),
            pltpu.VMEM((2, tm * blocks * half, 128), F32),
            dma((2,)), dma((blocks,)),
            dma((blocks,)), dma((blocks,)),
            dma((blocks,)), dma((blocks,)),
            dma((blocks,)), dma((blocks,)),
            dma((tm,)), dma((tm,)),
            dma((blocks,)), dma((blocks,)),
            dma((tm,)), dma((tm,)),
        ],
        compiler_params=pltpu.CompilerParams(
            collective_id=0, has_side_effects=True, vmem_limit_bytes=56 * 1024 * 1024
        ),
    )(traces.reshape(128, length), jnp.asarray(hann), slot_col, ends, jnp.asarray(forward), jnp.asarray(lag))


def solution(mesh):
    in_specs = (P("tm", "pairs", None), P(), P("pairs", None))
    out_specs = P("tm", "pairs")
    return jax.shard_map(
        on_device, mesh=mesh, in_specs=in_specs, out_specs=out_specs, check_vma=False
    )
```

```python
import functools
import math

import jax
import jax.numpy as jnp
import ml_dtypes
import numpy as np
from jax import lax
from jax.experimental import pallas as pl
from jax.experimental.pallas import tpu as pltpu
from jax.sharding import PartitionSpec as P

F = 1536
FLO = 32
LAG = 1024
RADIX = 8
MESH = pl.DeviceIdType.MESH
F32 = jnp.float32
BF16 = jnp.bfloat16


def split(blocks, tm):
    bins_each = F // blocks
    chunks = max(1, bins_each // (16 * tm))
    while bins_each % (chunks * tm):
        chunks -= 1
    bins = bins_each // (chunks * tm)
    return bins_each, chunks, bins, -(-bins // 16) * 16


def tables(length, blocks, tm):
    bins_each, chunks, bins, half = split(blocks, tm)
    group = blocks // RADIX
    short = length // RADIX
    angles = 2.0 * np.pi * np.arange(length) / length
    cos_of = np.cos(angles).astype(np.float32).astype(ml_dtypes.bfloat16)
    sin_of = np.sin(angles).astype(np.float32).astype(ml_dtypes.bfloat16)
    block_ids = np.arange(blocks)
    first = block_ids // group + RADIX * (block_ids % group) * bins_each
    freqs = FLO + first[:, None] + RADIX * np.arange(bins_each)[None, :]
    phases = freqs[:, :, None] * np.arange(short)[None, None, :] % length
    forward = np.concatenate([cos_of[phases], sin_of[phases]], axis=1)

    inside = np.arange(half)
    value = np.arange(chunks * tm)[:, None] * bins + np.minimum(inside, bins - 1)[None, :]
    freq = freqs[block_ids[None, :, None], value[:, None, :]].reshape(chunks, 1, -1)
    valid = np.broadcast_to(inside < bins, (chunks, tm, blocks, half)).reshape(chunks, 1, -1)
    lag_phase = freq * np.arange(2 * LAG // tm)[None, :, None] % length
    zero = np.zeros((), ml_dtypes.bfloat16)
    lag = np.concatenate(
        [np.where(valid, cos_of[lag_phase], zero), np.where(valid, -sin_of[lag_phase], zero)], axis=2
    )
    return forward.astype(ml_dtypes.bfloat16), lag.astype(ml_dtypes.bfloat16)


def kernel(
    blocks, tm, scale,
    x_hbm, hann, slot_row, pairs, tab_hbm, lag_hbm, out,
    x, tab, lag, slot_col, ends, folded, water, spec_out, spec_in, water_in, ends_in, onehot, white,
    part_out, part_in, pack_out, pack_in, turn, total_out,
    local_sem, tab_sem, ends_s, ends_r, spec_s, spec_r, water_s, water_r,
    part_s, part_r, pack_s, pack_r, last_s, last_r,
):
    me, mine = lax.axis_index("pairs"), lax.axis_index("tm")
    bins_each, chunks, bins, half = split(blocks, tm)
    chunk = bins_each // chunks
    group = blocks // RADIX
    length = x.shape[1]
    short = length // RADIX
    stations = onehot.shape[1]

    x_copy = pltpu.make_async_copy(x_hbm, x, local_sem.at[0])
    lag_copy = pltpu.make_async_copy(lag_hbm, lag, local_sem.at[1])
    x_copy.start()

    def step_of(i):
        return 1 + (i + blocks // 2 - 1) % (blocks - 1)

    def table_copy(s):
        return pltpu.make_async_copy(tab_hbm.at[(me + s) % blocks], tab.at[s], tab_sem.at[s])

    def start_table(i, c):
        table_copy(step_of(i)).start()
        return c

    lax.fori_loop(0, blocks - 1, start_table, 0)
    table_copy(0).start()
    lag_copy.start()

    def on_pairs(device):
        return {"pairs": device}

    def on_tm(device):
        return {"tm": device}

    ends[...] = jnp.zeros_like(ends)
    ends[0:1, 0:64] = pairs[0:1, :].astype(F32)
    ends[0:1, 64:128] = pairs[1:2, :].astype(F32)

    barrier = pltpu.get_barrier_semaphore()
    for s in range(1, blocks):
        pl.semaphore_signal(barrier, inc=1, device_id=on_pairs((me + s) % blocks), device_id_type=MESH)
    for s in range(1, tm):
        pl.semaphore_signal(barrier, inc=1, device_id=on_tm((mine + s) % tm), device_id_type=MESH)
    pl.semaphore_wait(barrier, blocks + tm - 2)

    def remote(src, dst, send, recv, device):
        return pltpu.make_async_remote_copy(
            src_ref=src, dst_ref=dst, send_sem=send, recv_sem=recv, device_id=device, device_id_type=MESH
        )

    def ends_copy(s):
        return remote(ends, ends_in.at[me], ends_s.at[s], ends_r.at[s], on_pairs((me + s) % blocks))

    def spec_copy(c, s):
        to = on_pairs((me + s) % blocks)
        return remote(spec_out.at[c, s], spec_in.at[c, me], spec_s.at[c, s], spec_r.at[c, s], to)

    def water_copy(s):
        return remote(water, water_in.at[me], water_s.at[s], water_r.at[s], on_pairs((me + s) % blocks))

    def part_copy(c, s):
        to = (mine + s) % tm
        return remote(part_out.at[c, to], part_in.at[c, mine], part_s.at[c, s], part_r.at[c, s], on_tm(to))

    def pack_copy(c, s):
        to = (me + s) % blocks
        return remote(pack_out.at[c, to], pack_in.at[c, mine, me], pack_s.at[c, s], pack_r.at[c, s], on_pairs(to))

    def last_copy(c, s):
        to = on_tm((mine + s) % tm)
        return remote(pack_in.at[c, mine], pack_in.at[c, mine], last_s.at[c, s], last_r.at[c, s], to)

    def each(low, high, act):
        def body(s, c):
            act(s)
            return c
        lax.fori_loop(low, high, body, 0)

    each(1, blocks, lambda s: ends_copy(s).start())
    ends_in[me] = ends[...]

    x_copy.wait()
    root = math.sqrt(0.5)

    def fold(i, c):
        low = pl.ds(pl.multiple_of(i * 16, 16), 16)
        high = pl.ds(pl.multiple_of(128 + i * 16, 16), 16)
        mean = jnp.sum(x[low, :], axis=1, keepdims=True) * (1.0 / length)
        for k in range(short // 128):
            v = []
            for q in range(RADIX):
                cols = slice(q * short + k * 128, q * short + (k + 1) * 128)
                v.append((x[low, cols] - mean) * hann[q:q + 1, k * 128:(k + 1) * 128])
            u = [v[q] + v[q + 4] for q in range(4)]
            d = [v[q] - v[q + 4] for q in range(4)]
            dm, dp = root * (d[1] - d[3]), root * (d[1] + d[3])
            even, odd = u[0] + u[2], u[1] + u[3]
            a2, b2 = u[0] - u[2], u[3] - u[1]
            a1, b1 = d[0] + dm, -d[2] - dp
            a3, b3 = d[0] - dm, d[2] - dp
            zero = jnp.zeros_like(even)
            classes = [
                (even + odd, zero), (a1, b1), (a2, b2), (a3, b3),
                (even - odd, zero), (a3, -b3), (a2, -b2), (a1, -b1),
            ]
            cols = slice(k * 128, (k + 1) * 128)
            for r, (a, b) in enumerate(classes):
                folded[r, low, cols] = a.astype(BF16)
                folded[r, high, cols] = b.astype(BF16)
        return c

    lax.fori_loop(0, 8, fold, 0)
    water[...] = jnp.zeros_like(water)

    def spectrum(s):
        table_copy(s).wait()
        to = (me + s) % blocks
        product = lax.dot_general(
            tab[s], folded[to // group], (((1,), (1,)), ((), ())), preferred_element_type=F32
        )
        re = product[:bins_each, :128] + product[bins_each:, 128:]
        im = product[:bins_each, 128:] - product[bins_each:, :128]
        water[...] += jnp.broadcast_to(jnp.sum(re * re + im * im, axis=0, keepdims=True), water.shape)
        return re.astype(BF16), im.astype(BF16)

    def send_block(i, c):
        s = step_of(i)
        re, im = spectrum(s)
        for part in range(chunks):
            spec_out[part, s, :chunk] = re[part * chunk:(part + 1) * chunk]
            spec_out[part, s, chunk:] = im[part * chunk:(part + 1) * chunk]
        spec_copy(0, s).start()
        return c

    lax.fori_loop(0, blocks - 1, send_block, 0)
    re, im = spectrum(0)
    for part in range(chunks):
        spec_in[part, me, :chunk] = re[part * chunk:(part + 1) * chunk]
        spec_in[part, me, chunk:] = im[part * chunk:(part + 1) * chunk]
    water_in[me] = water[...]
    each(1, blocks, lambda s: water_copy(s).start())
    for part in range(1, chunks):
        each(0, blocks - 1, lambda i: spec_copy(part, step_of(i)).start())

    for k in range(stations // 128):
        cols = slice(k * 128, (k + 1) * 128)
        slot_col[cols, :] = jnp.broadcast_to(slot_row[0:1, cols].astype(F32), (128, 128)).T
    lane = lax.broadcasted_iota(jnp.int32, (1, 128), 1)
    row_ids = lax.broadcasted_iota(jnp.int32, (stations, 256), 0).astype(F32)
    each(1, blocks, lambda s: ends_copy(s).wait())

    def swap(v):
        return pltpu.roll(v, 64, 1)

    def pick(g, c):
        a, b = ends_in[2 * g], ends_in[2 * g + 1]
        left = jnp.where(lane < 64, a, swap(b))[0:1]
        right = jnp.where(lane < 64, swap(a), b)[0:1]
        names = jnp.concatenate([left, right], axis=1)
        slots = jnp.concatenate([slot_col[...], slot_col[...]], axis=1)
        slots = jnp.sum(jnp.where(row_ids == names, slots, 0.0), axis=0, keepdims=True)
        onehot[g] = jnp.where(row_ids == slots, 1.0, 0.0).astype(BF16)
        return c

    lax.fori_loop(0, blocks // 2, pick, 0)

    first_lag = mine * (2 * LAG // tm) - LAG
    inner = lax.broadcasted_iota(jnp.int32, (half, 128), 0).astype(F32)

    def phase_turn(i, c):
        share, block = i // blocks, i % blocks
        base = FLO + block // group + RADIX * ((block % group) * bins_each + share * bins)
        product = (base.astype(F32) + RADIX * inner) * first_lag.astype(F32)
        phase = product - jnp.floor(product * (1.0 / length)) * length
        angle = phase * (2.0 * math.pi / length)
        sine = jnp.sin(angle)
        at = pl.ds(pl.multiple_of(i * half, half), half)
        turn[0, at, :] = jnp.cos(angle)
        turn[1, at, :] = jnp.where(lane < 64, -sine, sine)
        return c

    if half > bins:
        part_out[...] = jnp.zeros_like(part_out)

    def cross_chunk(part):
        def whiten(src):
            re = spec_in[part, src, :chunk].astype(F32)
            im = spec_in[part, src, chunk:].astype(F32)
            level = water_in[src][0:1] * (0.1 / F) + 1e-6
            factor = lax.rsqrt(re * re + im * im + level)
            return re * factor, im * factor

        def whiten_two(q, c):
            cols = pl.ds(pl.multiple_of(q * 128, 128), 128)
            one, two = whiten(2 * q), whiten(2 * q + 1)
            for k in range(2):
                first = jnp.where(lane < 64, one[k], swap(two[k]))
                second = jnp.where(lane < 64, swap(one[k]), two[k])
                at = k * chunk
                white[at:at + chunk, cols] = first.astype(BF16)
                at += 2 * chunk
                white[at:at + chunk, cols] = second.astype(BF16)
            return c

        lax.fori_loop(0, blocks // 2, whiten_two, 0)

        def cross(g, c):
            got = jnp.dot(white[...], onehot[g], preferred_element_type=F32)
            real = imag = None
            for w in range(2):
                at = 2 * w * chunk
                lr, rr = got[at:at + chunk, :128], got[at:at + chunk, 128:]
                at += chunk
                li, ri = got[at:at + chunk, :128], got[at:at + chunk, 128:]
                re, im = lr * rr + li * ri, li * rr - lr * ri
                real = re if real is None else real + re
                imag = im if imag is None else imag + im
            for t in range(tm):
                rows = slice(t * bins, (t + 1) * bins)
                part_out[part, t, g, :bins] = real[rows].astype(BF16)
                part_out[part, t, g, half:half + bins] = imag[rows].astype(BF16)
            return c

        lax.fori_loop(0, blocks // 2, cross, 0)
        each(1, tm, lambda s: part_copy(part, s).start())
        part_in[part, mine] = part_out[part, mine]

    def pack_chunk(part):
        each(1, tm, lambda s: part_copy(part, s).wait())

        def pack(g, c):
            total = part_in[part, 0, g].astype(F32)
            for t in range(1, tm):
                total += part_in[part, t, g].astype(F32)
            top, bottom = total[:half], total[half:]
            pack_out[part, 2 * g] = jnp.where(lane < 64, top, swap(bottom)).astype(BF16)
            pack_out[part, 2 * g + 1] = jnp.where(lane < 64, swap(top), bottom).astype(BF16)
            return c

        lax.fori_loop(0, blocks // 2, pack, 0)
        each(1, blocks, lambda s: pack_copy(part, s).start())
        pack_in[part, mine, me] = pack_out[part, me]

    def share_chunk(part):
        each(1, blocks, lambda s: pack_copy(part, s).wait())
        each(1, tm, lambda s: last_copy(part, s).start())

    def lag_chunk(part):
        each(1, tm, lambda s: last_copy(part, s).wait())
        count = tm * blocks * half
        at = slice(part * count, (part + 1) * count)
        stacked = pack_in[part].reshape(count, 128).astype(F32)
        turned = stacked * turn[0, at, :] + swap(stacked) * turn[1, at, :]
        values = jnp.concatenate([turned, swap(turned)], axis=0).astype(BF16)
        product = jnp.dot(lag[part], values, preferred_element_type=F32)
        total_out[...] = product if part == 0 else total_out[...] + product

    each(1, blocks, lambda s: water_copy(s).wait())
    for part in range(chunks):
        each(1, blocks, lambda s: spec_copy(part, s).wait())
        cross_chunk(part)
        if part == 0:
            lax.fori_loop(0, chunks * tm * blocks, phase_turn, 0)
            lag_copy.wait()
        else:
            share_chunk(part - 1)
        pack_chunk(part)
    for part in range(chunks - 1):
        lag_chunk(part)
    share_chunk(chunks - 1)
    lag_chunk(chunks - 1)
    out[...] = (total_out[...] * scale).T[:64]


def on_device(traces, station_slot, pair_stations):
    held, stations_each, length = traces.shape
    stations = station_slot.shape[0]
    blocks, tm = lax.axis_size("pairs"), lax.axis_size("tm")
    pairs_each = pair_stations.shape[0]
    assert held * stations_each == 128 and held == 2 and pairs_each == 64 and blocks % RADIX == 0
    bins_each, chunks, bins, half = split(blocks, tm)
    short = length // RADIX
    values = tm * blocks * half
    lag_rows = 2 * LAG // tm
    forward, lag = tables(length, blocks, tm)
    times = (np.arange(length, dtype=np.float64) + 0.5) * (2.0 * np.pi / length)
    hann = (0.5 - 0.5 * np.cos(times)).astype(np.float32).reshape(RADIX, short)
    scale = 1.0 / math.sqrt(F * held * tm)
    vmem = pl.BlockSpec(memory_space=pltpu.VMEM)
    anywhere = pl.BlockSpec(memory_space=pl.ANY)
    dma = pltpu.SemaphoreType.DMA
    result = pl.pallas_call(
        functools.partial(kernel, blocks, tm, scale),
        out_shape=jax.ShapeDtypeStruct((pairs_each, lag_rows), F32),
        in_specs=[anywhere, vmem, vmem, vmem, anywhere, anywhere],
        out_specs=vmem,
        scratch_shapes=[
            pltpu.VMEM((128, length), F32),
            pltpu.VMEM((blocks, 2 * bins_each, short), BF16),
            pltpu.VMEM((chunks, lag_rows, 2 * values), BF16),
            pltpu.VMEM((stations, 128), F32),
            pltpu.VMEM((8, 128), F32),
            pltpu.VMEM((RADIX, 256, short), BF16),
            pltpu.VMEM((8, 128), F32),
            pltpu.VMEM((chunks, blocks, 2 * bins_each // chunks, 128), BF16),
            pltpu.VMEM((chunks, blocks, 2 * bins_each // chunks, 128), BF16),
            pltpu.VMEM((blocks, 8, 128), F32),
            pltpu.VMEM((blocks, 8, 128), F32),
            pltpu.VMEM((blocks // 2, stations, 256), BF16),
            pltpu.VMEM((4 * bins_each // chunks, stations), BF16),
            pltpu.VMEM((chunks, tm, blocks // 2, 2 * half, 128), BF16),
            pltpu.VMEM((chunks, tm, blocks // 2, 2 * half, 128), BF16),
            pltpu.VMEM((chunks, blocks, half, 128), BF16),
            pltpu.VMEM((chunks, tm, blocks, half, 128), BF16),
            pltpu.VMEM((2, chunks * values, 128), F32),
            pltpu.VMEM((lag_rows, 128), F32),
            dma((2,)), dma((blocks,)),
            dma((blocks,)), dma((blocks,)),
            dma((chunks, blocks)), dma((chunks, blocks)),
            dma((blocks,)), dma((blocks,)),
            dma((chunks, tm)), dma((chunks, tm)),
            dma((chunks, blocks)), dma((chunks, blocks)),
            dma((chunks, tm)), dma((chunks, tm)),
        ],
        compiler_params=pltpu.CompilerParams(
            collective_id=0, has_side_effects=True, vmem_limit_bytes=56 * 1024 * 1024
        ),
    )(
        traces.reshape(128, length), jnp.asarray(hann), station_slot.reshape(1, stations),
        pair_stations.T, jnp.asarray(forward), jnp.asarray(lag),
    )
    return result.T


def solution(mesh):
    in_specs = (P("tm", "pairs", None), P(), P("pairs", None))
    out_specs = P("tm", "pairs")
    return jax.shard_map(
        on_device, mesh=mesh, in_specs=in_specs, out_specs=out_specs, check_vma=False
    )
```

```python
import functools
import math

import jax
import jax.numpy as jnp
import ml_dtypes
import numpy as np
from jax import lax
from jax.experimental import pallas as pl
from jax.experimental.pallas import tpu as pltpu
from jax.sharding import PartitionSpec as P

F = 1536
FLO = 32
LAG = 1024
RADIX = 8
MESH = pl.DeviceIdType.MESH
F32 = jnp.float32
BF16 = jnp.bfloat16


def split(blocks, tm):
    bins_each = F // blocks
    chunks = max(1, bins_each // (16 * tm))
    while bins_each % (chunks * tm):
        chunks -= 1
    bins = bins_each // (chunks * tm)
    return bins_each, chunks, bins, -(-bins // 16) * 16


def tables(length, blocks, tm):
    bins_each, chunks, bins, half = split(blocks, tm)
    group = blocks // RADIX
    short = length // RADIX
    angles = 2.0 * np.pi * np.arange(length) / length
    cos_of = np.cos(angles).astype(np.float32).astype(ml_dtypes.bfloat16)
    sin_of = np.sin(angles).astype(np.float32).astype(ml_dtypes.bfloat16)
    block_ids = np.arange(blocks)
    first = block_ids // group + RADIX * (block_ids % group) * bins_each
    freqs = FLO + first[:, None] + RADIX * np.arange(bins_each)[None, :]
    phases = freqs[:, :, None] * np.arange(short)[None, None, :] % length
    forward = np.concatenate([cos_of[phases], sin_of[phases]], axis=1)

    inside = np.arange(half)
    value = np.arange(chunks * tm)[:, None] * bins + np.minimum(inside, bins - 1)[None, :]
    freq = freqs[block_ids[None, :, None], value[:, None, :]].reshape(chunks, 1, -1)
    valid = np.broadcast_to(inside < bins, (chunks, tm, blocks, half)).reshape(chunks, 1, -1)
    lag_phase = freq * np.arange(2 * LAG // tm)[None, :, None] % length
    zero = np.zeros((), ml_dtypes.bfloat16)
    lag = np.concatenate(
        [np.where(valid, cos_of[lag_phase], zero), np.where(valid, -sin_of[lag_phase], zero)], axis=2
    )
    first_lag = np.arange(tm) * (2 * LAG // tm) - LAG
    turn_angle = 2.0 * np.pi / length * (freq.reshape(1, -1) * first_lag[:, None] % length)
    cosine, sine = np.cos(turn_angle), np.sin(turn_angle)
    turn = np.stack([np.stack([cosine, cosine], axis=2), np.stack([-sine, sine], axis=2)], axis=1)
    turn = np.repeat(turn.astype(np.float32), 64, axis=3)
    return forward.astype(ml_dtypes.bfloat16), lag.astype(ml_dtypes.bfloat16), turn


def kernel(
    blocks, tm, scale,
    x_hbm, hann, slot_row, pairs, tab_hbm, lag_hbm, turn_hbm, out,
    x, tab, lag, slot_col, ends, folded, water, spec_out, spec_in, water_in, ends_in, onehot, white,
    part_out, part_in, pack_out, pack_in, turn, total_out,
    local_sem, tab_sem, ends_s, ends_r, spec_s, spec_r, water_s, water_r,
    part_s, part_r, pack_s, pack_r, last_s, last_r,
):
    me, mine = lax.axis_index("pairs"), lax.axis_index("tm")
    bins_each, chunks, bins, half = split(blocks, tm)
    chunk = bins_each // chunks
    group = blocks // RADIX
    length = x.shape[1]
    short = length // RADIX
    stations = onehot.shape[1]

    x_copy = pltpu.make_async_copy(x_hbm, x, local_sem.at[0])
    lag_copy = pltpu.make_async_copy(lag_hbm, lag, local_sem.at[1])
    turn_copy = pltpu.make_async_copy(turn_hbm.at[mine], turn, local_sem.at[2])
    x_copy.start()

    def step_of(i):
        return 1 + (i + blocks // 2 - 1) % (blocks - 1)

    def table_copy(s):
        return pltpu.make_async_copy(tab_hbm.at[(me + s) % blocks], tab.at[s], tab_sem.at[s])

    def start_table(i, c):
        table_copy(step_of(i)).start()
        return c

    lax.fori_loop(0, blocks - 1, start_table, 0)
    table_copy(0).start()
    lag_copy.start()
    turn_copy.start()

    def on_pairs(device):
        return {"pairs": device}

    def on_tm(device):
        return {"tm": device}

    ends[...] = jnp.zeros_like(ends)
    ends[0:1, 0:64] = pairs[0:1, :].astype(F32)
    ends[0:1, 64:128] = pairs[1:2, :].astype(F32)

    barrier = pltpu.get_barrier_semaphore()
    for s in range(1, blocks):
        pl.semaphore_signal(barrier, inc=1, device_id=on_pairs((me + s) % blocks), device_id_type=MESH)
    for s in range(1, tm):
        pl.semaphore_signal(barrier, inc=1, device_id=on_tm((mine + s) % tm), device_id_type=MESH)
    def remote(src, dst, send, recv, device):
        return pltpu.make_async_remote_copy(
            src_ref=src, dst_ref=dst, send_sem=send, recv_sem=recv, device_id=device, device_id_type=MESH
        )

    def ends_copy(s):
        return remote(ends, ends_in.at[me], ends_s.at[s], ends_r.at[s], on_pairs((me + s) % blocks))

    def spec_copy(c, s):
        to = on_pairs((me + s) % blocks)
        return remote(spec_out.at[c, s], spec_in.at[c, me], spec_s.at[c, s], spec_r.at[c, s], to)

    def water_copy(s):
        return remote(water, water_in.at[me], water_s.at[s], water_r.at[s], on_pairs((me + s) % blocks))

    def part_copy(c, s):
        to = (mine + s) % tm
        return remote(part_out.at[c, to], part_in.at[c, mine], part_s.at[c, s], part_r.at[c, s], on_tm(to))

    def pack_copy(c, s):
        to = (me + s) % blocks
        return remote(pack_out.at[c, to], pack_in.at[c, mine, me], pack_s.at[c, s], pack_r.at[c, s], on_pairs(to))

    def last_copy(c, s):
        to = on_tm((mine + s) % tm)
        return remote(pack_in.at[c, mine], pack_in.at[c, mine], last_s.at[c, s], last_r.at[c, s], to)

    def each(low, high, act):
        def body(s, c):
            act(s)
            return c
        lax.fori_loop(low, high, body, 0)

    x_copy.wait()
    root = math.sqrt(0.5)

    def fold(i, c):
        low = pl.ds(pl.multiple_of(i * 16, 16), 16)
        high = pl.ds(pl.multiple_of(128 + i * 16, 16), 16)
        mean = jnp.sum(x[low, :], axis=1, keepdims=True) * (1.0 / length)
        for k in range(short // 128):
            v = []
            for q in range(RADIX):
                cols = slice(q * short + k * 128, q * short + (k + 1) * 128)
                v.append((x[low, cols] - mean) * hann[q:q + 1, k * 128:(k + 1) * 128])
            u = [v[q] + v[q + 4] for q in range(4)]
            d = [v[q] - v[q + 4] for q in range(4)]
            dm, dp = root * (d[1] - d[3]), root * (d[1] + d[3])
            even, odd = u[0] + u[2], u[1] + u[3]
            a2, b2 = u[0] - u[2], u[3] - u[1]
            a1, b1 = d[0] + dm, -d[2] - dp
            a3, b3 = d[0] - dm, d[2] - dp
            zero = jnp.zeros_like(even)
            classes = [
                (even + odd, zero), (a1, b1), (a2, b2), (a3, b3),
                (even - odd, zero), (a3, -b3), (a2, -b2), (a1, -b1),
            ]
            cols = slice(k * 128, (k + 1) * 128)
            for r, (a, b) in enumerate(classes):
                folded[r, low, cols] = a.astype(BF16)
                folded[r, high, cols] = b.astype(BF16)
        return c

    lax.fori_loop(0, 8, fold, 0)
    water[...] = jnp.zeros_like(water)

    pl.semaphore_wait(barrier, blocks + tm - 2)
    each(1, blocks, lambda s: ends_copy(s).start())
    ends_in[me] = ends[...]

    def spectrum(s):
        table_copy(s).wait()
        to = (me + s) % blocks
        product = lax.dot_general(
            tab[s], folded[to // group], (((1,), (1,)), ((), ())), preferred_element_type=F32
        )
        re = product[:bins_each, :128] + product[bins_each:, 128:]
        im = product[:bins_each, 128:] - product[bins_each:, :128]
        water[...] += jnp.broadcast_to(jnp.sum(re * re + im * im, axis=0, keepdims=True), water.shape)
        return re.astype(BF16), im.astype(BF16)

    def send_block(i, c):
        s = step_of(i)
        re, im = spectrum(s)
        for part in range(chunks):
            spec_out[part, s, :chunk] = re[part * chunk:(part + 1) * chunk]
            spec_out[part, s, chunk:] = im[part * chunk:(part + 1) * chunk]
        spec_copy(0, s).start()
        return c

    lax.fori_loop(0, blocks - 1, send_block, 0)
    re, im = spectrum(0)
    for part in range(chunks):
        spec_in[part, me, :chunk] = re[part * chunk:(part + 1) * chunk]
        spec_in[part, me, chunk:] = im[part * chunk:(part + 1) * chunk]
    water_in[me] = water[...]
    each(1, blocks, lambda s: water_copy(s).start())

    def send_next(part):
        def body(i, c):
            s = step_of(i)
            spec_copy(part, s).wait_send()
            if part + 1 < chunks:
                spec_copy(part + 1, s).start()
            return c
        lax.fori_loop(0, blocks - 1, body, 0)

    for k in range(stations // 128):
        cols = slice(k * 128, (k + 1) * 128)
        slot_col[cols, :] = jnp.broadcast_to(slot_row[0:1, cols].astype(F32), (128, 128)).T
    lane = lax.broadcasted_iota(jnp.int32, (1, 128), 1)
    row_ids = lax.broadcasted_iota(jnp.int32, (stations, 256), 0).astype(F32)
    each(1, blocks, lambda s: ends_copy(s).wait())

    def swap(v):
        return pltpu.roll(v, 64, 1)

    def pick(g, c):
        a, b = ends_in[2 * g], ends_in[2 * g + 1]
        left = jnp.where(lane < 64, a, swap(b))[0:1]
        right = jnp.where(lane < 64, swap(a), b)[0:1]
        names = jnp.concatenate([left, right], axis=1)
        slots = jnp.concatenate([slot_col[...], slot_col[...]], axis=1)
        slots = jnp.sum(jnp.where(row_ids == names, slots, 0.0), axis=0, keepdims=True)
        onehot[g] = jnp.where(row_ids == slots, 1.0, 0.0).astype(BF16)
        return c

    lax.fori_loop(0, blocks // 2, pick, 0)

    if half > bins:
        part_out[...] = jnp.zeros_like(part_out)

    def cross_chunk(part):
        def whiten(src):
            re = spec_in[part, src, :chunk].astype(F32)
            im = spec_in[part, src, chunk:].astype(F32)
            level = water_in[src][0:1] * (0.1 / F) + 1e-6
            factor = lax.rsqrt(re * re + im * im + level)
            return re * factor, im * factor

        def whiten_two(q, c):
            cols = pl.ds(pl.multiple_of(q * 128, 128), 128)
            one, two = whiten(2 * q), whiten(2 * q + 1)
            for k in range(2):
                first = jnp.where(lane < 64, one[k], swap(two[k]))
                second = jnp.where(lane < 64, swap(one[k]), two[k])
                at = k * chunk
                white[at:at + chunk, cols] = first.astype(BF16)
                at += 2 * chunk
                white[at:at + chunk, cols] = second.astype(BF16)
            return c

        lax.fori_loop(0, blocks // 2, whiten_two, 0)

        def cross(g, c):
            got = jnp.dot(white[...], onehot[g], preferred_element_type=F32)
            real = imag = None
            for w in range(2):
                at = 2 * w * chunk
                lr, rr = got[at:at + chunk, :128], got[at:at + chunk, 128:]
                at += chunk
                li, ri = got[at:at + chunk, :128], got[at:at + chunk, 128:]
                re, im = lr * rr + li * ri, li * rr - lr * ri
                real = re if real is None else real + re
                imag = im if imag is None else imag + im
            for t in range(tm):
                rows = slice(t * bins, (t + 1) * bins)
                part_out[part, t, g, :bins] = real[rows].astype(BF16)
                part_out[part, t, g, half:half + bins] = imag[rows].astype(BF16)
            return c

        lax.fori_loop(0, blocks // 2, cross, 0)
        each(1, tm, lambda s: part_copy(part, s).start())
        part_in[part, mine] = part_out[part, mine]

    def pack_chunk(part):
        each(1, tm, lambda s: part_copy(part, s).wait())

        def pack(g, c):
            total = part_in[part, 0, g].astype(F32)
            for t in range(1, tm):
                total += part_in[part, t, g].astype(F32)
            top, bottom = total[:half], total[half:]
            pack_out[part, 2 * g] = jnp.where(lane < 64, top, swap(bottom)).astype(BF16)
            pack_out[part, 2 * g + 1] = jnp.where(lane < 64, swap(top), bottom).astype(BF16)
            return c

        lax.fori_loop(0, blocks // 2, pack, 0)
        each(1, blocks, lambda s: pack_copy(part, s).start())
        pack_in[part, mine, me] = pack_out[part, me]

    def share_chunk(part):
        each(1, blocks, lambda s: pack_copy(part, s).wait())
        each(1, tm, lambda s: last_copy(part, s).start())

    def lag_chunk(part):
        each(1, tm, lambda s: last_copy(part, s).wait())
        count = tm * blocks * half
        at = slice(part * count, (part + 1) * count)
        stacked = pack_in[part].reshape(count, 128).astype(F32)
        turned = stacked * turn[0, at, :] + swap(stacked) * turn[1, at, :]
        values = jnp.concatenate([turned, swap(turned)], axis=0).astype(BF16)
        product = jnp.dot(lag[part], values, preferred_element_type=F32)
        total_out[...] = product if part == 0 else total_out[...] + product

    send_next(0)
    each(1, blocks, lambda s: water_copy(s).wait())
    for part in range(chunks):
        each(1, blocks, lambda s: spec_copy(part, s).wait_recv())
        cross_chunk(part)
        if part == 0:
            lag_copy.wait()
            turn_copy.wait()
        else:
            share_chunk(part - 1)
        pack_chunk(part)
        if part + 1 < chunks:
            send_next(part + 1)
    for part in range(chunks - 1):
        lag_chunk(part)
    share_chunk(chunks - 1)
    lag_chunk(chunks - 1)
    out[...] = (total_out[...] * scale).T[:64]


def on_device(traces, station_slot, pair_stations):
    held, stations_each, length = traces.shape
    stations = station_slot.shape[0]
    blocks, tm = lax.axis_size("pairs"), lax.axis_size("tm")
    pairs_each = pair_stations.shape[0]
    assert held * stations_each == 128 and held == 2 and pairs_each == 64 and blocks % RADIX == 0
    bins_each, chunks, bins, half = split(blocks, tm)
    short = length // RADIX
    values = tm * blocks * half
    lag_rows = 2 * LAG // tm
    forward, lag, turn = tables(length, blocks, tm)
    times = (np.arange(length, dtype=np.float64) + 0.5) * (2.0 * np.pi / length)
    hann = (0.5 - 0.5 * np.cos(times)).astype(np.float32).reshape(RADIX, short)
    scale = 1.0 / math.sqrt(F * held * tm)
    vmem = pl.BlockSpec(memory_space=pltpu.VMEM)
    anywhere = pl.BlockSpec(memory_space=pl.ANY)
    dma = pltpu.SemaphoreType.DMA
    result = pl.pallas_call(
        functools.partial(kernel, blocks, tm, scale),
        out_shape=jax.ShapeDtypeStruct((pairs_each, lag_rows), F32),
        in_specs=[anywhere, vmem, vmem, vmem, anywhere, anywhere, anywhere],
        out_specs=vmem,
        scratch_shapes=[
            pltpu.VMEM((128, length), F32),
            pltpu.VMEM((blocks, 2 * bins_each, short), BF16),
            pltpu.VMEM((chunks, lag_rows, 2 * values), BF16),
            pltpu.VMEM((stations, 128), F32),
            pltpu.VMEM((8, 128), F32),
            pltpu.VMEM((RADIX, 256, short), BF16),
            pltpu.VMEM((8, 128), F32),
            pltpu.VMEM((chunks, blocks, 2 * bins_each // chunks, 128), BF16),
            pltpu.VMEM((chunks, blocks, 2 * bins_each // chunks, 128), BF16),
            pltpu.VMEM((blocks, 8, 128), F32),
            pltpu.VMEM((blocks, 8, 128), F32),
            pltpu.VMEM((blocks // 2, stations, 256), BF16),
            pltpu.VMEM((4 * bins_each // chunks, stations), BF16),
            pltpu.VMEM((chunks, tm, blocks // 2, 2 * half, 128), BF16),
            pltpu.VMEM((chunks, tm, blocks // 2, 2 * half, 128), BF16),
            pltpu.VMEM((chunks, blocks, half, 128), BF16),
            pltpu.VMEM((chunks, tm, blocks, half, 128), BF16),
            pltpu.VMEM((2, chunks * values, 128), F32),
            pltpu.VMEM((lag_rows, 128), F32),
            dma((3,)), dma((blocks,)),
            dma((blocks,)), dma((blocks,)),
            dma((chunks, blocks)), dma((chunks, blocks)),
            dma((blocks,)), dma((blocks,)),
            dma((chunks, tm)), dma((chunks, tm)),
            dma((chunks, blocks)), dma((chunks, blocks)),
            dma((chunks, tm)), dma((chunks, tm)),
        ],
        compiler_params=pltpu.CompilerParams(
            collective_id=0, has_side_effects=True, vmem_limit_bytes=56 * 1024 * 1024
        ),
    )(
        traces.reshape(128, length), jnp.asarray(hann), station_slot.reshape(1, stations),
        pair_stations.T, jnp.asarray(forward), jnp.asarray(lag), jnp.asarray(turn),
    )
    return result.T


def solution(mesh):
    in_specs = (P("tm", "pairs", None), P(), P("pairs", None))
    out_specs = P("tm", "pairs")
    return jax.shard_map(
        on_device, mesh=mesh, in_specs=in_specs, out_specs=out_specs, check_vma=False
    )
```

```python
import functools
import math

import jax
import jax.numpy as jnp
import ml_dtypes
import numpy as np
from jax import lax
from jax.experimental import pallas as pl
from jax.experimental.pallas import tpu as pltpu
from jax.sharding import PartitionSpec as P

F = 1536
FLO = 32
LAG = 1024
RADIX = 8
MESH = pl.DeviceIdType.MESH
F32 = jnp.float32
BF16 = jnp.bfloat16


def split(blocks, tm):
    bins_each = F // blocks
    chunks = max(1, bins_each // (16 * tm))
    while bins_each % (chunks * tm):
        chunks -= 1
    bins = bins_each // (chunks * tm)
    return bins_each, chunks, bins, -(-bins // 16) * 16


def tables(length, blocks, tm):
    bins_each, chunks, bins, half = split(blocks, tm)
    group = blocks // RADIX
    short = length // RADIX
    angles = 2.0 * np.pi * np.arange(length) / length
    cos_of = np.cos(angles).astype(np.float32).astype(ml_dtypes.bfloat16)
    sin_of = np.sin(angles).astype(np.float32).astype(ml_dtypes.bfloat16)
    block_ids = np.arange(blocks)
    first = block_ids // group + RADIX * (block_ids % group) * bins_each
    freqs = FLO + first[:, None] + RADIX * np.arange(bins_each)[None, :]
    phases = freqs[:, :, None] * np.arange(short)[None, None, :] % length
    forward = np.concatenate([cos_of[phases], sin_of[phases]], axis=1)

    inside = np.arange(half)
    value = np.arange(chunks * tm)[:, None] * bins + np.minimum(inside, bins - 1)[None, :]
    freq = freqs[block_ids[None, :, None], value[:, None, :]].reshape(chunks, 1, -1)
    valid = np.broadcast_to(inside < bins, (chunks, tm, blocks, half)).reshape(chunks, 1, -1)
    lag_phase = freq * np.arange(2 * LAG // tm)[None, :, None] % length
    zero = np.zeros((), ml_dtypes.bfloat16)
    lag = np.concatenate(
        [np.where(valid, cos_of[lag_phase], zero), np.where(valid, -sin_of[lag_phase], zero)], axis=2
    )
    first_lag = np.arange(tm) * (2 * LAG // tm) - LAG
    turn_angle = 2.0 * np.pi / length * (freq.reshape(1, -1) * first_lag[:, None] % length)
    cosine, sine = np.cos(turn_angle), np.sin(turn_angle)
    turn = np.stack([np.stack([cosine, cosine], axis=2), np.stack([-sine, sine], axis=2)], axis=1)
    turn = np.repeat(turn.astype(np.float32), 64, axis=3)
    return forward.astype(ml_dtypes.bfloat16), lag.astype(ml_dtypes.bfloat16), turn


def kernel(
    blocks, tm,
    x_hbm, hann_hbm, slot_hbm, pairs_hbm, tab_hbm, lag_hbm, turn_hbm, out,
    x, hann, slot_row, pairs, tab, lag, slot_col, ends, folded, water, spec_out, spec_in, water_in, ends_in, onehot, white,
    part_out, part_in, pack_out, pack_in, turn, total_out,
    local_sem, x_sem, tab_sem, ends_s, ends_r, spec_s, spec_r, water_s, water_r,
    part_s, part_r, pack_s, pack_r, last_s, last_r,
):
    me, mine = lax.axis_index("pairs"), lax.axis_index("tm")
    bins_each, chunks, bins, half = split(blocks, tm)
    chunk = bins_each // chunks
    group = blocks // RADIX
    length = x.shape[1]
    short = length // RADIX
    stations = onehot.shape[1]

    lag_copy = pltpu.make_async_copy(lag_hbm, lag, local_sem.at[0])
    turn_copy = pltpu.make_async_copy(turn_hbm.at[mine], turn, local_sem.at[1])
    hann_copy = pltpu.make_async_copy(hann_hbm, hann, local_sem.at[2])
    slot_copy = pltpu.make_async_copy(slot_hbm, slot_row, local_sem.at[3])
    pairs_copy = pltpu.make_async_copy(pairs_hbm, pairs, local_sem.at[4])

    def x_copy(i):
        at = pl.ds(pl.multiple_of(i * 16, 16), 16)
        return pltpu.make_async_copy(x_hbm.at[at], x.at[at], x_sem.at[i])

    hann_copy.start()
    x_copy(0).start()
    pairs_copy.start()
    slot_copy.start()

    def step_of(i):
        return 1 + (i + blocks // 2 - 1) % (blocks - 1)

    def table_copy(s):
        return pltpu.make_async_copy(tab_hbm.at[(me + s) % blocks], tab.at[s], tab_sem.at[s])

    def on_pairs(device):
        return {"pairs": device}

    def on_tm(device):
        return {"tm": device}

    barrier = pltpu.get_barrier_semaphore()
    for s in range(1, blocks):
        pl.semaphore_signal(barrier, inc=1, device_id=on_pairs((me + s) % blocks), device_id_type=MESH)
    for s in range(1, tm):
        pl.semaphore_signal(barrier, inc=1, device_id=on_tm((mine + s) % tm), device_id_type=MESH)
    for i in range(1, 8):
        x_copy(i).start()

    def remote(src, dst, send, recv, device):
        return pltpu.make_async_remote_copy(
            src_ref=src, dst_ref=dst, send_sem=send, recv_sem=recv, device_id=device, device_id_type=MESH
        )

    def ends_copy(s):
        return remote(ends, ends_in.at[me], ends_s.at[s], ends_r.at[s], on_pairs((me + s) % blocks))

    def spec_copy(c, s):
        to = on_pairs((me + s) % blocks)
        return remote(spec_out.at[c, s], spec_in.at[c, me], spec_s.at[c, s], spec_r.at[c, s], to)

    def water_copy(s):
        return remote(water, water_in.at[me], water_s.at[s], water_r.at[s], on_pairs((me + s) % blocks))

    def part_copy(c, s):
        to = (mine + s) % tm
        return remote(part_out.at[c, to], part_in.at[c, mine], part_s.at[c, s], part_r.at[c, s], on_tm(to))

    def pack_copy(c, s):
        to = (me + s) % blocks
        return remote(pack_out.at[c, to], pack_in.at[c, mine, me], pack_s.at[c, s], pack_r.at[c, s], on_pairs(to))

    def last_copy(c, s):
        to = on_tm((mine + s) % tm)
        return remote(pack_in.at[c, mine], pack_in.at[c, mine], last_s.at[c, s], last_r.at[c, s], to)

    def each(low, high, act):
        def body(s, c):
            act(s)
            return c
        lax.fori_loop(low, high, body, 0)

    hann_copy.wait()
    root = math.sqrt(0.5)

    def fold(i, c):
        low = pl.ds(pl.multiple_of(i * 16, 16), 16)
        high = pl.ds(pl.multiple_of(128 + i * 16, 16), 16)
        x_copy(i).wait()
        for k in range(group):
            at = i * group + k
            table_copy(jnp.where(at < blocks - 1, step_of(at), 0)).start()
        mean = jnp.sum(x[low, :], axis=1, keepdims=True) * (1.0 / length)
        for k in range(short // 128):
            v = []
            for q in range(RADIX):
                cols = slice(q * short + k * 128, q * short + (k + 1) * 128)
                v.append((x[low, cols] - mean) * hann[q:q + 1, k * 128:(k + 1) * 128])
            u = [v[q] + v[q + 4] for q in range(4)]
            d = [v[q] - v[q + 4] for q in range(4)]
            dm, dp = root * (d[1] - d[3]), root * (d[1] + d[3])
            even, odd = u[0] + u[2], u[1] + u[3]
            a2, b2 = u[0] - u[2], u[3] - u[1]
            a1, b1 = d[0] + dm, -d[2] - dp
            a3, b3 = d[0] - dm, d[2] - dp
            zero = jnp.zeros_like(even)
            classes = [
                (even + odd, zero), (a1, b1), (a2, b2), (a3, b3),
                (even - odd, zero), (a3, -b3), (a2, -b2), (a1, -b1),
            ]
            cols = slice(k * 128, (k + 1) * 128)
            for r, (a, b) in enumerate(classes):
                folded[r, low, cols] = a.astype(BF16)
                folded[r, high, cols] = b.astype(BF16)
        return c

    lax.fori_loop(0, 8, fold, 0)
    water[...] = jnp.zeros_like(water)

    pl.semaphore_wait(barrier, blocks + tm - 2)
    pairs_copy.wait()
    ends[...] = jnp.zeros_like(ends)
    ends[0:1, 0:64] = pairs[0:1, :].astype(F32)
    ends[0:1, 64:128] = pairs[1:2, :].astype(F32)
    each(1, blocks, lambda s: ends_copy(s).start())
    ends_in[me] = ends[...]

    def spectrum(s):
        table_copy(s).wait()
        to = (me + s) % blocks
        product = lax.dot_general(
            tab[s], folded[to // group], (((1,), (1,)), ((), ())), preferred_element_type=F32
        )
        re = product[:bins_each, :128] + product[bins_each:, 128:]
        im = product[:bins_each, 128:] - product[bins_each:, :128]
        water[...] += jnp.broadcast_to(jnp.sum(re * re + im * im, axis=0, keepdims=True), water.shape)
        return re.astype(BF16), im.astype(BF16)

    def send_block(i, c):
        s = step_of(i)
        re, im = spectrum(s)
        for part in range(chunks):
            spec_out[part, s, :chunk] = re[part * chunk:(part + 1) * chunk]
            spec_out[part, s, chunk:] = im[part * chunk:(part + 1) * chunk]
        spec_copy(0, s).start()
        return c

    lax.fori_loop(0, blocks - 1, send_block, 0)
    re, im = spectrum(0)
    for part in range(chunks):
        spec_in[part, me, :chunk] = re[part * chunk:(part + 1) * chunk]
        spec_in[part, me, chunk:] = im[part * chunk:(part + 1) * chunk]
    water_in[me] = water[...]
    each(1, blocks, lambda s: water_copy(s).start())

    def send_next(part):
        def body(i, c):
            s = step_of(i)
            spec_copy(part, s).wait_send()
            if part + 1 < chunks:
                spec_copy(part + 1, s).start()
            return c
        lax.fori_loop(0, blocks - 1, body, 0)

    slot_copy.wait()
    for k in range(stations // 128):
        cols = slice(k * 128, (k + 1) * 128)
        slot_col[cols, :] = jnp.broadcast_to(slot_row[0:1, cols].astype(F32), (128, 128)).T
    lane = lax.broadcasted_iota(jnp.int32, (1, 128), 1)
    row_ids = lax.broadcasted_iota(jnp.int32, (stations, 256), 0).astype(F32)
    each(1, blocks, lambda s: ends_copy(s).wait())

    def swap(v):
        return pltpu.roll(v, 64, 1)

    def pick(g, c):
        a, b = ends_in[2 * g], ends_in[2 * g + 1]
        left = jnp.where(lane < 64, a, swap(b))[0:1]
        right = jnp.where(lane < 64, swap(a), b)[0:1]
        names = jnp.concatenate([left, right], axis=1)
        slots = jnp.concatenate([slot_col[...], slot_col[...]], axis=1)
        slots = jnp.sum(jnp.where(row_ids == names, slots, 0.0), axis=0, keepdims=True)
        onehot[g] = jnp.where(row_ids == slots, 1.0, 0.0).astype(BF16)
        return c

    lax.fori_loop(0, blocks // 2, pick, 0)

    if half > bins:
        part_out[...] = jnp.zeros_like(part_out)

    def cross_chunk(part):
        def whiten(src):
            re = spec_in[part, src, :chunk].astype(F32)
            im = spec_in[part, src, chunk:].astype(F32)
            level = water_in[src][0:1] * (0.1 / F) + 1e-6
            factor = lax.rsqrt(re * re + im * im + level)
            return re * factor, im * factor

        def whiten_two(q, c):
            cols = pl.ds(pl.multiple_of(q * 128, 128), 128)
            one, two = whiten(2 * q), whiten(2 * q + 1)
            for k in range(2):
                first = jnp.where(lane < 64, one[k], swap(two[k]))
                second = jnp.where(lane < 64, swap(one[k]), two[k])
                at = k * chunk
                white[at:at + chunk, cols] = first.astype(BF16)
                at += 2 * chunk
                white[at:at + chunk, cols] = second.astype(BF16)
            return c

        lax.fori_loop(0, blocks // 2, whiten_two, 0)

        def cross(g, c):
            got = jnp.dot(white[...], onehot[g], preferred_element_type=F32)
            real = imag = None
            for w in range(2):
                at = 2 * w * chunk
                lr, rr = got[at:at + chunk, :128], got[at:at + chunk, 128:]
                at += chunk
                li, ri = got[at:at + chunk, :128], got[at:at + chunk, 128:]
                re, im = lr * rr + li * ri, li * rr - lr * ri
                real = re if real is None else real + re
                imag = im if imag is None else imag + im
            for t in range(tm):
                rows = slice(t * bins, (t + 1) * bins)
                part_out[part, t, g, :bins] = real[rows].astype(BF16)
                part_out[part, t, g, half:half + bins] = imag[rows].astype(BF16)
            return c

        lax.fori_loop(0, blocks // 2, cross, 0)
        each(1, tm, lambda s: part_copy(part, s).start())
        part_in[part, mine] = part_out[part, mine]

    def pack_chunk(part):
        each(1, tm, lambda s: part_copy(part, s).wait())

        def pack(g, c):
            total = part_in[part, 0, g].astype(F32)
            for t in range(1, tm):
                total += part_in[part, t, g].astype(F32)
            top, bottom = total[:half], total[half:]
            pack_out[part, 2 * g] = jnp.where(lane < 64, top, swap(bottom)).astype(BF16)
            pack_out[part, 2 * g + 1] = jnp.where(lane < 64, swap(top), bottom).astype(BF16)
            return c

        lax.fori_loop(0, blocks // 2, pack, 0)
        each(1, blocks, lambda s: pack_copy(part, s).start())
        pack_in[part, mine, me] = pack_out[part, me]

    def share_chunk(part):
        each(1, blocks, lambda s: pack_copy(part, s).wait())
        each(1, tm, lambda s: last_copy(part, s).start())

    def lag_chunk(part):
        each(1, tm, lambda s: last_copy(part, s).wait())
        count = tm * blocks * half
        at = slice(part * count, (part + 1) * count)
        stacked = pack_in[part].reshape(count, 128).astype(F32)
        turned = stacked * turn[0, at, :] + swap(stacked) * turn[1, at, :]
        values = jnp.concatenate([turned, swap(turned)], axis=0).astype(BF16)
        product = jnp.dot(lag[part], values, preferred_element_type=F32)
        total_out[...] = product if part == 0 else total_out[...] + product

    lag_copy.start()
    turn_copy.start()
    send_next(0)
    each(1, blocks, lambda s: water_copy(s).wait())
    for part in range(chunks):
        each(1, blocks, lambda s: spec_copy(part, s).wait_recv())
        cross_chunk(part)
        if part + 1 < chunks:
            send_next(part + 1)
        if part == 0:
            lag_copy.wait()
            turn_copy.wait()
        else:
            share_chunk(part - 1)
        pack_chunk(part)
    for part in range(chunks - 1):
        lag_chunk(part)
    share_chunk(chunks - 1)
    lag_chunk(chunks - 1)
    out[...] = total_out[...].T[:64]


def on_device(traces, station_slot, pair_stations):
    held, stations_each, length = traces.shape
    stations = station_slot.shape[0]
    blocks, tm = lax.axis_size("pairs"), lax.axis_size("tm")
    pairs_each = pair_stations.shape[0]
    assert held * stations_each == 128 and held == 2 and pairs_each == 64 and blocks % RADIX == 0
    bins_each, chunks, bins, half = split(blocks, tm)
    short = length // RADIX
    values = tm * blocks * half
    lag_rows = 2 * LAG // tm
    forward, lag, turn = tables(length, blocks, tm)
    times = (np.arange(length, dtype=np.float64) + 0.5) * (2.0 * np.pi / length)
    hann = (0.5 - 0.5 * np.cos(times)).astype(np.float32).reshape(RADIX, short)
    scale = 1.0 / math.sqrt(F * held * tm)
    vmem = pl.BlockSpec(memory_space=pltpu.VMEM)
    anywhere = pl.BlockSpec(memory_space=pl.ANY)
    dma = pltpu.SemaphoreType.DMA
    result = pl.pallas_call(
        functools.partial(kernel, blocks, tm),
        out_shape=jax.ShapeDtypeStruct((pairs_each, lag_rows), F32),
        in_specs=[anywhere, anywhere, anywhere, anywhere, anywhere, anywhere, anywhere],
        out_specs=vmem,
        scratch_shapes=[
            pltpu.VMEM((128, length), F32),
            pltpu.VMEM((RADIX, short), F32),
            pltpu.VMEM((1, stations), jnp.int32),
            pltpu.VMEM((2, pairs_each), jnp.int32),
            pltpu.VMEM((blocks, 2 * bins_each, short), BF16),
            pltpu.VMEM((chunks, lag_rows, 2 * values), BF16),
            pltpu.VMEM((stations, 128), F32),
            pltpu.VMEM((8, 128), F32),
            pltpu.VMEM((RADIX, 256, short), BF16),
            pltpu.VMEM((8, 128), F32),
            pltpu.VMEM((chunks, blocks, 2 * bins_each // chunks, 128), BF16),
            pltpu.VMEM((chunks, blocks, 2 * bins_each // chunks, 128), BF16),
            pltpu.VMEM((blocks, 8, 128), F32),
            pltpu.VMEM((blocks, 8, 128), F32),
            pltpu.VMEM((blocks // 2, stations, 256), BF16),
            pltpu.VMEM((4 * bins_each // chunks, stations), BF16),
            pltpu.VMEM((chunks, tm, blocks // 2, 2 * half, 128), BF16),
            pltpu.VMEM((chunks, tm, blocks // 2, 2 * half, 128), BF16),
            pltpu.VMEM((chunks, blocks, half, 128), BF16),
            pltpu.VMEM((chunks, tm, blocks, half, 128), BF16),
            pltpu.VMEM((2, chunks * values, 128), F32),
            pltpu.VMEM((lag_rows, 128), F32),
            dma((5,)), dma((8,)), dma((blocks,)),
            dma((blocks,)), dma((blocks,)),
            dma((chunks, blocks)), dma((chunks, blocks)),
            dma((blocks,)), dma((blocks,)),
            dma((chunks, tm)), dma((chunks, tm)),
            dma((chunks, blocks)), dma((chunks, blocks)),
            dma((chunks, tm)), dma((chunks, tm)),
        ],
        compiler_params=pltpu.CompilerParams(
            collective_id=0, has_side_effects=True, vmem_limit_bytes=56 * 1024 * 1024
        ),
    )(
        traces.reshape(128, length), jnp.asarray(hann), station_slot.reshape(1, stations),
        pair_stations.T, jnp.asarray(forward), jnp.asarray(lag), jnp.asarray(turn),
    )
    return result.T * scale


def solution(mesh):
    in_specs = (P("tm", "pairs", None), P(), P("pairs", None))
    out_specs = P("tm", "pairs")
    return jax.shard_map(
        on_device, mesh=mesh, in_specs=in_specs, out_specs=out_specs, check_vma=False
    )
```

```python
import functools
import math

import jax
import jax.numpy as jnp
import ml_dtypes
import numpy as np
from jax import lax
from jax.experimental import pallas as pl
from jax.experimental.pallas import tpu as pltpu
from jax.sharding import PartitionSpec as P

F = 1536
FLO = 32
LAG = 1024
RADIX = 8
CORES = 2
MESH = pl.DeviceIdType.MESH
F32 = jnp.float32
BF16 = jnp.bfloat16


def split(blocks, tm):
    bins_each = F // blocks
    chunks = max(1, bins_each // (16 * tm))
    while bins_each % (chunks * tm):
        chunks -= 1
    bins = bins_each // (chunks * tm)
    return bins_each, chunks, bins, -(-bins // 16) * 16


def tables(length, blocks, tm):
    bins_each, chunks, bins, half = split(blocks, tm)
    group = blocks // RADIX
    short = length // RADIX
    angles = 2.0 * np.pi * np.arange(length) / length
    cos_of = np.cos(angles).astype(np.float32).astype(ml_dtypes.bfloat16)
    sin_of = np.sin(angles).astype(np.float32).astype(ml_dtypes.bfloat16)
    block_ids = np.arange(blocks)
    first = block_ids // group + RADIX * (block_ids % group) * bins_each
    freqs = FLO + first[:, None] + RADIX * np.arange(bins_each)[None, :]
    phases = freqs[:, :, None] * np.arange(short)[None, None, :] % length
    forward = np.concatenate([cos_of[phases], sin_of[phases]], axis=1)

    inside = np.arange(half)
    value = np.arange(chunks * tm)[:, None] * bins + np.minimum(inside, bins - 1)[None, :]
    freq = freqs[block_ids[None, :, None], value[:, None, :]].reshape(chunks, 1, -1)
    valid = np.broadcast_to(inside < bins, (chunks, tm, blocks, half)).reshape(chunks, 1, -1)
    lag_phase = freq * np.arange(2 * LAG // tm)[None, :, None] % length
    zero = np.zeros((), ml_dtypes.bfloat16)
    lag = np.concatenate(
        [np.where(valid, cos_of[lag_phase], zero), np.where(valid, -sin_of[lag_phase], zero)], axis=2
    )
    first_lag = np.arange(tm) * (2 * LAG // tm) - LAG
    turn_angle = 2.0 * np.pi / length * (freq.reshape(1, -1) * first_lag[:, None] % length)
    cosine, sine = np.cos(turn_angle), np.sin(turn_angle)
    turn = np.stack([np.stack([cosine, cosine], axis=2), np.stack([-sine, sine], axis=2)], axis=1)
    turn = np.repeat(turn.astype(np.float32), 64, axis=3)
    return forward.astype(ml_dtypes.bfloat16), lag.astype(ml_dtypes.bfloat16), turn


def kernel(
    blocks, tm,
    x_hbm, hann_hbm, slot_hbm, pairs_hbm, tab_hbm, lag_hbm, turn_hbm, out,
    x, hann, slot_row, pairs, tab, lag, slot_col, ends, folded, water, spec_out, spec_in, water_in, ends_in, onehot, white,
    part_out, part_in, pack_out, pack_in, turn, total_out,
    local_sem, x_sem, tab_sem, ends_s, ends_r, spec_s, spec_r, water_s, water_r,
    part_s, part_r, pack_s, pack_r, last_s, last_r,
    wide_s, wide_r, core_s, core_r,
):
    me, mine = lax.axis_index("pairs"), lax.axis_index("tm")
    bins_each, chunks, bins, half = split(blocks, tm)
    chunk = bins_each // chunks
    chips = tm // CORES
    group = blocks // RADIX
    length = x.shape[1]
    short = length // RADIX
    stations = onehot.shape[1]

    lag_copy = pltpu.make_async_copy(lag_hbm, lag, local_sem.at[0])
    turn_copy = pltpu.make_async_copy(turn_hbm.at[mine], turn, local_sem.at[1])
    hann_copy = pltpu.make_async_copy(hann_hbm, hann, local_sem.at[2])
    slot_copy = pltpu.make_async_copy(slot_hbm, slot_row, local_sem.at[3])
    pairs_copy = pltpu.make_async_copy(pairs_hbm, pairs, local_sem.at[4])

    def x_copy(i):
        at = pl.ds(pl.multiple_of(i * 16, 16), 16)
        return pltpu.make_async_copy(x_hbm.at[at], x.at[at], x_sem.at[i])

    hann_copy.start()
    x_copy(0).start()
    pairs_copy.start()
    slot_copy.start()

    def step_of(i):
        return 1 + (i + blocks // 2 - 1) % (blocks - 1)

    def table_copy(s):
        return pltpu.make_async_copy(tab_hbm.at[(me + s) % blocks], tab.at[s], tab_sem.at[s])

    def on_pairs(device):
        return {"pairs": device}

    def on_tm(device):
        return {"tm": device}

    def wide(s):
        return {"pairs": (me + s) % blocks, "tm": (mine + CORES * (s // blocks)) % tm}

    barrier = pltpu.get_barrier_semaphore()
    for s in range(1, blocks):
        pl.semaphore_signal(barrier, inc=1, device_id=on_pairs((me + s) % blocks), device_id_type=MESH)
    for s in range(1, tm):
        pl.semaphore_signal(barrier, inc=1, device_id=on_tm((mine + s) % tm), device_id_type=MESH)
    for s in range(blocks, blocks * chips):
        if s % blocks:
            pl.semaphore_signal(barrier, inc=1, device_id=wide(s), device_id_type=MESH)
    for i in range(1, 8):
        x_copy(i).start()

    def remote(src, dst, send, recv, device):
        return pltpu.make_async_remote_copy(
            src_ref=src, dst_ref=dst, send_sem=send, recv_sem=recv, device_id=device, device_id_type=MESH
        )

    def ends_copy(s):
        return remote(ends, ends_in.at[me], ends_s.at[s], ends_r.at[s], on_pairs((me + s) % blocks))

    def spec_copy(c, s):
        to = on_pairs((me + s) % blocks)
        return remote(spec_out.at[c, s], spec_in.at[c, me], spec_s.at[c, s], spec_r.at[c, s], to)

    def water_copy(s):
        return remote(water, water_in.at[me], water_s.at[s], water_r.at[s], on_pairs((me + s) % blocks))

    def part_copy(c, s):
        to = (mine + s) % tm
        return remote(part_out.at[c, to], part_in.at[c, mine], part_s.at[c, s], part_r.at[c, s], on_tm(to))

    def pack_copy(c, s):
        to = (me + s) % blocks
        return remote(pack_out.at[c, to], pack_in.at[c, mine, me], pack_s.at[c, s], pack_r.at[c, s], on_pairs(to))

    def last_copy(c, s):
        to = on_tm((mine + s) % tm)
        return remote(pack_in.at[c, mine], pack_in.at[c, mine], last_s.at[c, s], last_r.at[c, s], to)

    def wide_copy(s):
        c, to = chunks - 1, (me + s) % blocks
        return remote(pack_out.at[c, to], pack_in.at[c, mine, me], wide_s.at[s], wide_r.at[s], wide(s))

    def core_copy(k):
        core = mine % CORES
        at = pack_in.at[chunks - 1, CORES * k + core]
        return remote(at, at, core_s.at[k], core_r.at[k], on_tm(mine + 1 - 2 * core))

    def each(low, high, act):
        def body(s, c):
            act(s)
            return c
        lax.fori_loop(low, high, body, 0)

    hann_copy.wait()
    root = math.sqrt(0.5)

    def fold(i, c):
        low = pl.ds(pl.multiple_of(i * 16, 16), 16)
        high = pl.ds(pl.multiple_of(128 + i * 16, 16), 16)
        x_copy(i).wait()
        for k in range(group):
            at = i * group + k
            table_copy(jnp.where(at < blocks - 1, step_of(at), 0)).start()
        mean = jnp.sum(x[low, :], axis=1, keepdims=True) * (1.0 / length)
        for k in range(short // 128):
            v = []
            for q in range(RADIX):
                cols = slice(q * short + k * 128, q * short + (k + 1) * 128)
                v.append((x[low, cols] - mean) * hann[q:q + 1, k * 128:(k + 1) * 128])
            u = [v[q] + v[q + 4] for q in range(4)]
            d = [v[q] - v[q + 4] for q in range(4)]
            dm, dp = root * (d[1] - d[3]), root * (d[1] + d[3])
            even, odd = u[0] + u[2], u[1] + u[3]
            a2, b2 = u[0] - u[2], u[3] - u[1]
            a1, b1 = d[0] + dm, -d[2] - dp
            a3, b3 = d[0] - dm, d[2] - dp
            zero = jnp.zeros_like(even)
            classes = [
                (even + odd, zero), (a1, b1), (a2, b2), (a3, b3),
                (even - odd, zero), (a3, -b3), (a2, -b2), (a1, -b1),
            ]
            cols = slice(k * 128, (k + 1) * 128)
            for r, (a, b) in enumerate(classes):
                folded[r, low, cols] = a.astype(BF16)
                folded[r, high, cols] = b.astype(BF16)
        return c

    lax.fori_loop(0, 8, fold, 0)
    water[...] = jnp.zeros_like(water)

    pl.semaphore_wait(barrier, (blocks - 1) * chips + tm - 1)
    pairs_copy.wait()
    ends[...] = jnp.zeros_like(ends)
    ends[0:1, 0:64] = pairs[0:1, :].astype(F32)
    ends[0:1, 64:128] = pairs[1:2, :].astype(F32)
    each(1, blocks, lambda s: ends_copy(s).start())
    ends_in[me] = ends[...]

    def spectrum(s):
        table_copy(s).wait()
        to = (me + s) % blocks
        product = lax.dot_general(
            tab[s], folded[to // group], (((1,), (1,)), ((), ())), preferred_element_type=F32
        )
        re = product[:bins_each, :128] + product[bins_each:, 128:]
        im = product[:bins_each, 128:] - product[bins_each:, :128]
        water[...] += jnp.broadcast_to(jnp.sum(re * re + im * im, axis=0, keepdims=True), water.shape)
        return re.astype(BF16), im.astype(BF16)

    def send_block(i, c):
        s = step_of(i)
        re, im = spectrum(s)
        for part in range(chunks):
            spec_out[part, s, :chunk] = re[part * chunk:(part + 1) * chunk]
            spec_out[part, s, chunk:] = im[part * chunk:(part + 1) * chunk]
        spec_copy(0, s).start()
        return c

    lax.fori_loop(0, blocks - 1, send_block, 0)
    re, im = spectrum(0)
    for part in range(chunks):
        spec_in[part, me, :chunk] = re[part * chunk:(part + 1) * chunk]
        spec_in[part, me, chunk:] = im[part * chunk:(part + 1) * chunk]
    water_in[me] = water[...]
    each(1, blocks, lambda s: water_copy(s).start())

    def send_next(part):
        def body(i, c):
            s = step_of(i)
            spec_copy(part, s).wait_send()
            if part + 1 < chunks:
                spec_copy(part + 1, s).start()
            return c
        lax.fori_loop(0, blocks - 1, body, 0)

    slot_copy.wait()
    for k in range(stations // 128):
        cols = slice(k * 128, (k + 1) * 128)
        slot_col[cols, :] = jnp.broadcast_to(slot_row[0:1, cols].astype(F32), (128, 128)).T
    lane = lax.broadcasted_iota(jnp.int32, (1, 128), 1)
    row_ids = lax.broadcasted_iota(jnp.int32, (stations, 256), 0).astype(F32)
    each(1, blocks, lambda s: ends_copy(s).wait())

    def swap(v):
        return pltpu.roll(v, 64, 1)

    def pick(g, c):
        a, b = ends_in[2 * g], ends_in[2 * g + 1]
        left = jnp.where(lane < 64, a, swap(b))[0:1]
        right = jnp.where(lane < 64, swap(a), b)[0:1]
        names = jnp.concatenate([left, right], axis=1)
        slots = jnp.concatenate([slot_col[...], slot_col[...]], axis=1)
        slots = jnp.sum(jnp.where(row_ids == names, slots, 0.0), axis=0, keepdims=True)
        onehot[g] = jnp.where(row_ids == slots, 1.0, 0.0).astype(BF16)
        return c

    lax.fori_loop(0, blocks // 2, pick, 0)

    if half > bins:
        part_out[...] = jnp.zeros_like(part_out)

    def cross_chunk(part):
        def whiten(src):
            re = spec_in[part, src, :chunk].astype(F32)
            im = spec_in[part, src, chunk:].astype(F32)
            level = water_in[src][0:1] * (0.1 / F) + 1e-6
            factor = lax.rsqrt(re * re + im * im + level)
            return re * factor, im * factor

        def whiten_two(q, c):
            cols = pl.ds(pl.multiple_of(q * 128, 128), 128)
            one, two = whiten(2 * q), whiten(2 * q + 1)
            for k in range(2):
                first = jnp.where(lane < 64, one[k], swap(two[k]))
                second = jnp.where(lane < 64, swap(one[k]), two[k])
                at = k * chunk
                white[at:at + chunk, cols] = first.astype(BF16)
                at += 2 * chunk
                white[at:at + chunk, cols] = second.astype(BF16)
            return c

        lax.fori_loop(0, blocks // 2, whiten_two, 0)

        def cross(g, c):
            got = jnp.dot(white[...], onehot[g], preferred_element_type=F32)
            real = imag = None
            for w in range(2):
                at = 2 * w * chunk
                lr, rr = got[at:at + chunk, :128], got[at:at + chunk, 128:]
                at += chunk
                li, ri = got[at:at + chunk, :128], got[at:at + chunk, 128:]
                re, im = lr * rr + li * ri, li * rr - lr * ri
                real = re if real is None else real + re
                imag = im if imag is None else imag + im
            for t in range(tm):
                rows = slice(t * bins, (t + 1) * bins)
                part_out[part, t, g, :bins] = real[rows].astype(BF16)
                part_out[part, t, g, half:half + bins] = imag[rows].astype(BF16)
            return c

        lax.fori_loop(0, blocks // 2, cross, 0)
        each(1, tm, lambda s: part_copy(part, s).start())
        part_in[part, mine] = part_out[part, mine]

    def pack_chunk(part):
        each(1, tm, lambda s: part_copy(part, s).wait())

        def pack(g, c):
            total = part_in[part, 0, g].astype(F32)
            for t in range(1, tm):
                total += part_in[part, t, g].astype(F32)
            top, bottom = total[:half], total[half:]
            pack_out[part, 2 * g] = jnp.where(lane < 64, top, swap(bottom)).astype(BF16)
            pack_out[part, 2 * g + 1] = jnp.where(lane < 64, swap(top), bottom).astype(BF16)
            return c

        lax.fori_loop(0, blocks // 2, pack, 0)
        if part == chunks - 1:
            each(1, blocks * chips, lambda s: wide_copy(s).start())
        else:
            each(1, blocks, lambda s: pack_copy(part, s).start())
        pack_in[part, mine, me] = pack_out[part, me]

    def share_chunk(part):
        if part == chunks - 1:
            each(1, blocks * chips, lambda s: wide_copy(s).wait())
            each(0, chips, lambda k: core_copy(k).start())
        else:
            each(1, blocks, lambda s: pack_copy(part, s).wait())
            each(1, tm, lambda s: last_copy(part, s).start())

    def lag_chunk(part):
        if part == chunks - 1:
            each(0, chips, lambda k: core_copy(k).wait())
        else:
            each(1, tm, lambda s: last_copy(part, s).wait())
        count = tm * blocks * half
        at = slice(part * count, (part + 1) * count)
        stacked = pack_in[part].reshape(count, 128).astype(F32)
        turned = stacked * turn[0, at, :] + swap(stacked) * turn[1, at, :]
        values = jnp.concatenate([turned, swap(turned)], axis=0).astype(BF16)
        product = jnp.dot(lag[part], values, preferred_element_type=F32)
        total_out[...] = product if part == 0 else total_out[...] + product

    lag_copy.start()
    turn_copy.start()
    send_next(0)
    each(1, blocks, lambda s: water_copy(s).wait())
    for part in range(chunks):
        each(1, blocks, lambda s: spec_copy(part, s).wait_recv())
        cross_chunk(part)
        if part + 1 < chunks:
            send_next(part + 1)
        if part == 0:
            lag_copy.wait()
            turn_copy.wait()
        else:
            share_chunk(part - 1)
        pack_chunk(part)
    for part in range(chunks - 1):
        lag_chunk(part)
    share_chunk(chunks - 1)
    lag_chunk(chunks - 1)
    out[...] = total_out[...].T[:64]


def on_device(traces, station_slot, pair_stations):
    held, stations_each, length = traces.shape
    stations = station_slot.shape[0]
    blocks, tm = lax.axis_size("pairs"), lax.axis_size("tm")
    pairs_each = pair_stations.shape[0]
    assert held * stations_each == 128 and held == 2 and pairs_each == 64 and blocks % RADIX == 0
    bins_each, chunks, bins, half = split(blocks, tm)
    short = length // RADIX
    values = tm * blocks * half
    lag_rows = 2 * LAG // tm
    forward, lag, turn = tables(length, blocks, tm)
    times = (np.arange(length, dtype=np.float64) + 0.5) * (2.0 * np.pi / length)
    hann = (0.5 - 0.5 * np.cos(times)).astype(np.float32).reshape(RADIX, short)
    scale = 1.0 / math.sqrt(F * held * tm)
    vmem = pl.BlockSpec(memory_space=pltpu.VMEM)
    anywhere = pl.BlockSpec(memory_space=pl.ANY)
    dma = pltpu.SemaphoreType.DMA
    result = pl.pallas_call(
        functools.partial(kernel, blocks, tm),
        out_shape=jax.ShapeDtypeStruct((pairs_each, lag_rows), F32),
        in_specs=[anywhere, anywhere, anywhere, anywhere, anywhere, anywhere, anywhere],
        out_specs=vmem,
        scratch_shapes=[
            pltpu.VMEM((128, length), F32),
            pltpu.VMEM((RADIX, short), F32),
            pltpu.VMEM((1, stations), jnp.int32),
            pltpu.VMEM((2, pairs_each), jnp.int32),
            pltpu.VMEM((blocks, 2 * bins_each, short), BF16),
            pltpu.VMEM((chunks, lag_rows, 2 * values), BF16),
            pltpu.VMEM((stations, 128), F32),
            pltpu.VMEM((8, 128), F32),
            pltpu.VMEM((RADIX, 256, short), BF16),
            pltpu.VMEM((8, 128), F32),
            pltpu.VMEM((chunks, blocks, 2 * bins_each // chunks, 128), BF16),
            pltpu.VMEM((chunks, blocks, 2 * bins_each // chunks, 128), BF16),
            pltpu.VMEM((blocks, 8, 128), F32),
            pltpu.VMEM((blocks, 8, 128), F32),
            pltpu.VMEM((blocks // 2, stations, 256), BF16),
            pltpu.VMEM((4 * bins_each // chunks, stations), BF16),
            pltpu.VMEM((chunks, tm, blocks // 2, 2 * half, 128), BF16),
            pltpu.VMEM((chunks, tm, blocks // 2, 2 * half, 128), BF16),
            pltpu.VMEM((chunks, blocks, half, 128), BF16),
            pltpu.VMEM((chunks, tm, blocks, half, 128), BF16),
            pltpu.VMEM((2, chunks * values, 128), F32),
            pltpu.VMEM((lag_rows, 128), F32),
            dma((5,)), dma((8,)), dma((blocks,)),
            dma((blocks,)), dma((blocks,)),
            dma((chunks, blocks)), dma((chunks, blocks)),
            dma((blocks,)), dma((blocks,)),
            dma((chunks, tm)), dma((chunks, tm)),
            dma((chunks, blocks)), dma((chunks, blocks)),
            dma((chunks, tm)), dma((chunks, tm)),
            dma((blocks * tm // CORES,)), dma((blocks * tm // CORES,)),
            dma((tm // CORES,)), dma((tm // CORES,)),
        ],
        compiler_params=pltpu.CompilerParams(
            collective_id=0, has_side_effects=True, vmem_limit_bytes=56 * 1024 * 1024
        ),
    )(
        traces.reshape(128, length), jnp.asarray(hann), station_slot.reshape(1, stations),
        pair_stations.T, jnp.asarray(forward), jnp.asarray(lag), jnp.asarray(turn),
    )
    return result.T * scale


def solution(mesh):
    in_specs = (P("tm", "pairs", None), P(), P("pairs", None))
    out_specs = P("tm", "pairs")
    return jax.shard_map(
        on_device, mesh=mesh, in_specs=in_specs, out_specs=out_specs, check_vma=False
    )
```

```python
import functools
import math

import jax
import jax.numpy as jnp
import ml_dtypes
import numpy as np
from jax import lax
from jax.experimental import pallas as pl
from jax.experimental.pallas import tpu as pltpu
from jax.sharding import PartitionSpec as P

F = 1536
FLO = 32
LAG = 1024
RADIX = 8
MESH = pl.DeviceIdType.MESH
F32 = jnp.float32
BF16 = jnp.bfloat16


def split(blocks, tm):
    bins_each = F // blocks
    chunks = max(1, bins_each // (16 * tm))
    while bins_each % (chunks * tm):
        chunks -= 1
    bins = bins_each // (chunks * tm)
    return bins_each, chunks, bins, -(-bins // 16) * 16


def tables(length, blocks, tm):
    bins_each, chunks, bins, half = split(blocks, tm)
    group = blocks // RADIX
    short = length // RADIX
    angles = 2.0 * np.pi * np.arange(length) / length
    cos_of = np.cos(angles).astype(np.float32).astype(ml_dtypes.bfloat16)
    sin_of = np.sin(angles).astype(np.float32).astype(ml_dtypes.bfloat16)
    block_ids = np.arange(blocks)
    first = block_ids // group + RADIX * (block_ids % group) * bins_each
    freqs = FLO + first[:, None] + RADIX * np.arange(bins_each)[None, :]
    phases = freqs[:, :, None] * np.arange(short)[None, None, :] % length
    forward = np.concatenate([cos_of[phases], sin_of[phases]], axis=1)

    inside = np.arange(half)
    value = np.arange(chunks * tm)[:, None] * bins + np.minimum(inside, bins - 1)[None, :]
    freq = freqs[block_ids[None, :, None], value[:, None, :]].reshape(chunks, 1, -1)
    valid = np.broadcast_to(inside < bins, (chunks, tm, blocks, half)).reshape(chunks, 1, -1)
    lag_phase = freq * np.arange(2 * LAG // tm)[None, :, None] % length
    zero = np.zeros((), ml_dtypes.bfloat16)
    lag = np.concatenate(
        [np.where(valid, cos_of[lag_phase], zero), np.where(valid, -sin_of[lag_phase], zero)], axis=2
    )
    first_lag = np.arange(tm) * (2 * LAG // tm) - LAG
    turn_angle = 2.0 * np.pi / length * (freq.reshape(1, -1) * first_lag[:, None] % length)
    cosine, sine = np.cos(turn_angle), np.sin(turn_angle)
    turn = np.stack([np.stack([cosine, cosine], axis=2), np.stack([-sine, sine], axis=2)], axis=1)
    turn = np.repeat(turn.astype(np.float32), 64, axis=3)
    return forward.astype(ml_dtypes.bfloat16), lag.astype(ml_dtypes.bfloat16), turn


def kernel(
    blocks, tm,
    x_hbm, hann_hbm, slot_hbm, pairs_hbm, tab_hbm, lag_hbm, turn_hbm, out,
    x, hann, slot_row, pairs, tab, lag, slot_col, ends, folded, water, spec_out, spec_in, water_in, ends_in, onehot, white,
    part_out, part_in, pack_out, pack_in, turn, total_out,
    local_sem, x_sem, tab_sem, ends_s, ends_r, spec_s, spec_r, water_s, water_r,
    part_s, part_r, pack_s, pack_r, last_s, last_r,
):
    me, mine = lax.axis_index("pairs"), lax.axis_index("tm")
    def wrapped(base, size):
        return [jnp.where(base + s >= size, base + s - size, base + s) for s in range(size)]

    block_at, tm_at = wrapped(me, blocks), wrapped(mine, tm)
    bins_each, chunks, bins, half = split(blocks, tm)
    chunk = bins_each // chunks
    group = blocks // RADIX
    length = x.shape[1]
    short = length // RADIX
    stations = onehot.shape[1]

    lag_copy = pltpu.make_async_copy(lag_hbm, lag, local_sem.at[0])
    turn_copy = pltpu.make_async_copy(turn_hbm.at[mine], turn, local_sem.at[1])
    hann_copy = pltpu.make_async_copy(hann_hbm, hann, local_sem.at[2])
    slot_copy = pltpu.make_async_copy(slot_hbm, slot_row, local_sem.at[3])
    pairs_copy = pltpu.make_async_copy(pairs_hbm, pairs, local_sem.at[4])

    def x_copy(i):
        at = pl.ds(pl.multiple_of(i * 16, 16), 16)
        return pltpu.make_async_copy(x_hbm.at[at], x.at[at], x_sem.at[i])

    hann_copy.start()
    x_copy(0).start()
    pairs_copy.start()
    slot_copy.start()

    def step_of(i):
        return 1 + (i + blocks // 2 - 1) % (blocks - 1)

    def table_copy(s):
        return pltpu.make_async_copy(tab_hbm.at[block_at[s]], tab.at[s], tab_sem.at[s])

    def on_pairs(device):
        return {"pairs": device}

    def on_tm(device):
        return {"tm": device}

    barrier = pltpu.get_barrier_semaphore()
    for s in range(1, blocks):
        pl.semaphore_signal(barrier, inc=1, device_id=on_pairs(block_at[s]), device_id_type=MESH)
    for s in range(1, tm):
        pl.semaphore_signal(barrier, inc=1, device_id=on_tm(tm_at[s]), device_id_type=MESH)
    for i in range(1, 8):
        x_copy(i).start()
    for i in range(blocks - 1):
        table_copy(step_of(i)).start()
    table_copy(0).start()

    def remote(src, dst, send, recv, device):
        return pltpu.make_async_remote_copy(
            src_ref=src, dst_ref=dst, send_sem=send, recv_sem=recv, device_id=device, device_id_type=MESH
        )

    def ends_copy(s):
        return remote(ends, ends_in.at[me], ends_s.at[s], ends_r.at[s], on_pairs(block_at[s]))

    def spec_copy(c, s):
        to = on_pairs(block_at[s])
        return remote(spec_out.at[c, s], spec_in.at[c, me], spec_s.at[c, s], spec_r.at[c, s], to)

    def water_copy(s):
        return remote(water, water_in.at[me], water_s.at[s], water_r.at[s], on_pairs(block_at[s]))

    def part_copy(c, s):
        to = tm_at[s]
        return remote(part_out.at[c, to], part_in.at[c, mine], part_s.at[c, s], part_r.at[c, s], on_tm(to))

    def pack_copy(c, s):
        to = block_at[s]
        return remote(pack_out.at[c, to], pack_in.at[c, mine, me], pack_s.at[c, s], pack_r.at[c, s], on_pairs(to))

    def last_copy(c, s):
        to = on_tm(tm_at[s])
        return remote(pack_in.at[c, mine], pack_in.at[c, mine], last_s.at[c, s], last_r.at[c, s], to)

    def each(low, high, act):
        for s in range(low, high):
            act(s)

    hann_copy.wait()
    root = math.sqrt(0.5)

    def fold(i, c):
        low = pl.ds(pl.multiple_of(i * 16, 16), 16)
        high = pl.ds(pl.multiple_of(128 + i * 16, 16), 16)
        x_copy(i).wait()
        mean = jnp.sum(x[low, :], axis=1, keepdims=True) * (1.0 / length)
        for k in range(short // 128):
            v = []
            for q in range(RADIX):
                cols = slice(q * short + k * 128, q * short + (k + 1) * 128)
                v.append((x[low, cols] - mean) * hann[q:q + 1, k * 128:(k + 1) * 128])
            u = [v[q] + v[q + 4] for q in range(4)]
            d = [v[q] - v[q + 4] for q in range(4)]
            dm, dp = root * (d[1] - d[3]), root * (d[1] + d[3])
            even, odd = u[0] + u[2], u[1] + u[3]
            a2, b2 = u[0] - u[2], u[3] - u[1]
            a1, b1 = d[0] + dm, -d[2] - dp
            a3, b3 = d[0] - dm, d[2] - dp
            zero = jnp.zeros_like(even)
            classes = [
                (even + odd, zero), (a1, b1), (a2, b2), (a3, b3),
                (even - odd, zero), (a3, -b3), (a2, -b2), (a1, -b1),
            ]
            cols = slice(k * 128, (k + 1) * 128)
            for r, (a, b) in enumerate(classes):
                folded[r, low, cols] = a.astype(BF16)
                folded[r, high, cols] = b.astype(BF16)
        return c

    lax.fori_loop(0, 8, fold, 0)
    water[...] = jnp.zeros_like(water)

    pl.semaphore_wait(barrier, blocks + tm - 2)
    pairs_copy.wait()
    ends[...] = jnp.zeros_like(ends)
    ends[0:1, 0:64] = pairs[0:1, :].astype(F32)
    ends[0:1, 64:128] = pairs[1:2, :].astype(F32)
    each(1, blocks, lambda s: ends_copy(s).start())
    ends_in[me] = ends[...]

    def spectrum(s):
        table_copy(s).wait()
        to = block_at[s]
        product = lax.dot_general(
            tab[s], folded[to // group], (((1,), (1,)), ((), ())), preferred_element_type=F32
        )
        re = product[:bins_each, :128] + product[bins_each:, 128:]
        im = product[:bins_each, 128:] - product[bins_each:, :128]
        water[...] += jnp.broadcast_to(jnp.sum(re * re + im * im, axis=0, keepdims=True), water.shape)
        return re.astype(BF16), im.astype(BF16)

    def send_block(s):
        re, im = spectrum(s)
        for part in range(chunks):
            spec_out[part, s, :chunk] = re[part * chunk:(part + 1) * chunk]
            spec_out[part, s, chunk:] = im[part * chunk:(part + 1) * chunk]
        spec_copy(0, s).start()

    for i in range(blocks - 1):
        send_block(step_of(i))
    re, im = spectrum(0)
    for part in range(chunks):
        spec_in[part, me, :chunk] = re[part * chunk:(part + 1) * chunk]
        spec_in[part, me, chunk:] = im[part * chunk:(part + 1) * chunk]
    water_in[me] = water[...]
    each(1, blocks, lambda s: water_copy(s).start())

    def send_next(part, low=0, high=blocks - 1):
        for i in range(low, high):
            s = step_of(i)
            spec_copy(part, s).wait_send()
            if part + 1 < chunks:
                spec_copy(part + 1, s).start()

    send_next(0, 0, blocks // 2)

    slot_copy.wait()
    for k in range(stations // 128):
        cols = slice(k * 128, (k + 1) * 128)
        slot_col[cols, :] = jnp.broadcast_to(slot_row[0:1, cols].astype(F32), (128, 128)).T
    lane = lax.broadcasted_iota(jnp.int32, (1, 128), 1)
    row_ids = lax.broadcasted_iota(jnp.int32, (stations, 256), 0).astype(F32)
    each(1, blocks, lambda s: ends_copy(s).wait())

    def swap(v):
        return pltpu.roll(v, 64, 1)

    def pick(g, c):
        a, b = ends_in[2 * g], ends_in[2 * g + 1]
        left = jnp.where(lane < 64, a, swap(b))[0:1]
        right = jnp.where(lane < 64, swap(a), b)[0:1]
        names = jnp.concatenate([left, right], axis=1)
        slots = jnp.concatenate([slot_col[...], slot_col[...]], axis=1)
        slots = jnp.sum(jnp.where(row_ids == names, slots, 0.0), axis=0, keepdims=True)
        onehot[g] = jnp.where(row_ids == slots, 1.0, 0.0).astype(BF16)
        return c

    lax.fori_loop(0, blocks // 2, pick, 0, unroll=2)

    if half > bins:
        part_out[...] = jnp.zeros_like(part_out)

    def cross_chunk(part):
        def whiten(src):
            re = spec_in[part, src, :chunk].astype(F32)
            im = spec_in[part, src, chunk:].astype(F32)
            level = water_in[src][0:1] * (0.1 / F) + 1e-6
            factor = lax.rsqrt(re * re + im * im + level)
            return re * factor, im * factor

        def whiten_two(q, c):
            cols = pl.ds(pl.multiple_of(q * 128, 128), 128)
            one, two = whiten(2 * q), whiten(2 * q + 1)
            for k in range(2):
                first = jnp.where(lane < 64, one[k], swap(two[k]))
                second = jnp.where(lane < 64, swap(one[k]), two[k])
                at = k * chunk
                white[at:at + chunk, cols] = first.astype(BF16)
                at += 2 * chunk
                white[at:at + chunk, cols] = second.astype(BF16)
            return c

        lax.fori_loop(0, blocks // 2, whiten_two, 0, unroll=2)

        def cross(g, c):
            got = jnp.dot(white[...], onehot[g], preferred_element_type=F32)
            real = imag = None
            for w in range(2):
                at = 2 * w * chunk
                lr, rr = got[at:at + chunk, :128], got[at:at + chunk, 128:]
                at += chunk
                li, ri = got[at:at + chunk, :128], got[at:at + chunk, 128:]
                re, im = lr * rr + li * ri, li * rr - lr * ri
                real = re if real is None else real + re
                imag = im if imag is None else imag + im
            for t in range(tm):
                rows = slice(t * bins, (t + 1) * bins)
                part_out[part, t, g, :bins] = real[rows].astype(BF16)
                part_out[part, t, g, half:half + bins] = imag[rows].astype(BF16)
            return c

        lax.fori_loop(0, blocks // 2, cross, 0, unroll=4)
        each(1, tm, lambda s: part_copy(part, s).start())
        part_in[part, mine] = part_out[part, mine]

    def pack_chunk(part):
        each(1, tm, lambda s: part_copy(part, s).wait())

        def pack(g, c):
            total = part_in[part, 0, g].astype(F32)
            for t in range(1, tm):
                total += part_in[part, t, g].astype(F32)
            top, bottom = total[:half], total[half:]
            pack_out[part, 2 * g] = jnp.where(lane < 64, top, swap(bottom)).astype(BF16)
            pack_out[part, 2 * g + 1] = jnp.where(lane < 64, swap(top), bottom).astype(BF16)
            return c

        lax.fori_loop(0, blocks // 2, pack, 0, unroll=4)
        each(1, blocks, lambda s: pack_copy(part, s).start())
        pack_in[part, mine, me] = pack_out[part, me]

    def share_chunk(part):
        each(1, blocks, lambda s: pack_copy(part, s).wait())
        each(1, tm, lambda s: last_copy(part, s).start())

    def lag_chunk(part):
        each(1, tm, lambda s: last_copy(part, s).wait())
        count = tm * blocks * half
        at = slice(part * count, (part + 1) * count)
        stacked = pack_in[part].reshape(count, 128).astype(F32)
        turned = stacked * turn[0, at, :] + swap(stacked) * turn[1, at, :]
        values = jnp.concatenate([turned, swap(turned)], axis=0).astype(BF16)
        product = jnp.dot(lag[part], values, preferred_element_type=F32)
        total_out[...] = product if part == 0 else total_out[...] + product

    lag_copy.start()
    turn_copy.start()
    send_next(0, blocks // 2)
    each(1, blocks, lambda s: water_copy(s).wait())
    for part in range(chunks):
        each(1, blocks, lambda s: spec_copy(part, s).wait_recv())
        cross_chunk(part)
        if part + 1 < chunks:
            send_next(part + 1)
        if part == 0:
            lag_copy.wait()
            turn_copy.wait()
        else:
            share_chunk(part - 1)
        pack_chunk(part)
    for part in range(chunks - 1):
        lag_chunk(part)
    share_chunk(chunks - 1)
    lag_chunk(chunks - 1)
    out[...] = total_out[...].T[:64]


def on_device(traces, station_slot, pair_stations):
    held, stations_each, length = traces.shape
    stations = station_slot.shape[0]
    blocks, tm = lax.axis_size("pairs"), lax.axis_size("tm")
    pairs_each = pair_stations.shape[0]
    assert held * stations_each == 128 and held == 2 and pairs_each == 64 and blocks % RADIX == 0
    bins_each, chunks, bins, half = split(blocks, tm)
    short = length // RADIX
    values = tm * blocks * half
    lag_rows = 2 * LAG // tm
    forward, lag, turn = tables(length, blocks, tm)
    times = (np.arange(length, dtype=np.float64) + 0.5) * (2.0 * np.pi / length)
    hann = (0.5 - 0.5 * np.cos(times)).astype(np.float32).reshape(RADIX, short)
    scale = 1.0 / math.sqrt(F * held * tm)
    vmem = pl.BlockSpec(memory_space=pltpu.VMEM)
    anywhere = pl.BlockSpec(memory_space=pl.ANY)
    dma = pltpu.SemaphoreType.DMA
    result = pl.pallas_call(
        functools.partial(kernel, blocks, tm),
        out_shape=jax.ShapeDtypeStruct((pairs_each, lag_rows), F32),
        in_specs=[anywhere, anywhere, anywhere, anywhere, anywhere, anywhere, anywhere],
        out_specs=vmem,
        scratch_shapes=[
            pltpu.VMEM((128, length), F32),
            pltpu.VMEM((RADIX, short), F32),
            pltpu.VMEM((1, stations), jnp.int32),
            pltpu.VMEM((2, pairs_each), jnp.int32),
            pltpu.VMEM((blocks, 2 * bins_each, short), BF16),
            pltpu.VMEM((chunks, lag_rows, 2 * values), BF16),
            pltpu.VMEM((stations, 128), F32),
            pltpu.VMEM((8, 128), F32),
            pltpu.VMEM((RADIX, 256, short), BF16),
            pltpu.VMEM((8, 128), F32),
            pltpu.VMEM((chunks, blocks, 2 * bins_each // chunks, 128), BF16),
            pltpu.VMEM((chunks, blocks, 2 * bins_each // chunks, 128), BF16),
            pltpu.VMEM((blocks, 8, 128), F32),
            pltpu.VMEM((blocks, 8, 128), F32),
            pltpu.VMEM((blocks // 2, stations, 256), BF16),
            pltpu.VMEM((4 * bins_each // chunks, stations), BF16),
            pltpu.VMEM((chunks, tm, blocks // 2, 2 * half, 128), BF16),
            pltpu.VMEM((chunks, tm, blocks // 2, 2 * half, 128), BF16),
            pltpu.VMEM((chunks, blocks, half, 128), BF16),
            pltpu.VMEM((chunks, tm, blocks, half, 128), BF16),
            pltpu.VMEM((2, chunks * values, 128), F32),
            pltpu.VMEM((lag_rows, 128), F32),
            dma((5,)), dma((8,)), dma((blocks,)),
            dma((blocks,)), dma((blocks,)),
            dma((chunks, blocks)), dma((chunks, blocks)),
            dma((blocks,)), dma((blocks,)),
            dma((chunks, tm)), dma((chunks, tm)),
            dma((chunks, blocks)), dma((chunks, blocks)),
            dma((chunks, tm)), dma((chunks, tm)),
        ],
        compiler_params=pltpu.CompilerParams(
            collective_id=0, has_side_effects=True, vmem_limit_bytes=56 * 1024 * 1024
        ),
    )(
        traces.reshape(128, length), jnp.asarray(hann), station_slot.reshape(1, stations),
        pair_stations.T, jnp.asarray(forward), jnp.asarray(lag), jnp.asarray(turn),
    )
    return result.T * scale


def solution(mesh):
    in_specs = (P("tm", "pairs", None), P(), P("pairs", None))
    out_specs = P("tm", "pairs")
    return jax.shard_map(
        on_device, mesh=mesh, in_specs=in_specs, out_specs=out_specs, check_vma=False
    )
```

```python
import functools
import math

import jax
import jax.numpy as jnp
import ml_dtypes
import numpy as np
from jax import lax
from jax.experimental import pallas as pl
from jax.experimental.pallas import tpu as pltpu
from jax.sharding import PartitionSpec as P

F = 1536
FLO = 32
LAG = 1024
RADIX = 8
MESH = pl.DeviceIdType.MESH
F32 = jnp.float32
BF16 = jnp.bfloat16


def split(blocks, tm):
    bins_each = F // blocks
    chunks = max(1, bins_each // (16 * tm))
    while bins_each % (chunks * tm):
        chunks -= 1
    bins = bins_each // (chunks * tm)
    return bins_each, chunks, bins, -(-bins // 16) * 16


def tables(length, blocks, tm):
    bins_each, chunks, bins, half = split(blocks, tm)
    group = blocks // RADIX
    short = length // RADIX
    angles = 2.0 * np.pi * np.arange(length) / length
    cos_of = np.cos(angles).astype(np.float32).astype(ml_dtypes.bfloat16)
    sin_of = np.sin(angles).astype(np.float32).astype(ml_dtypes.bfloat16)
    block_ids = np.arange(blocks)
    first = block_ids // group + RADIX * (block_ids % group) * bins_each
    freqs = FLO + first[:, None] + RADIX * np.arange(bins_each)[None, :]
    phases = freqs[:, :, None] * np.arange(short)[None, None, :] % length
    forward = np.concatenate([cos_of[phases], sin_of[phases]], axis=1)

    inside = np.arange(half)
    value = np.arange(chunks * tm)[:, None] * bins + np.minimum(inside, bins - 1)[None, :]
    freq = freqs[block_ids[None, :, None], value[:, None, :]].reshape(chunks, 1, -1)
    valid = np.broadcast_to(inside < bins, (chunks, tm, blocks, half)).reshape(chunks, 1, -1)
    lag_phase = freq * np.arange(2 * LAG // tm)[None, :, None] % length
    zero = np.zeros((), ml_dtypes.bfloat16)
    lag = np.concatenate(
        [np.where(valid, cos_of[lag_phase], zero), np.where(valid, -sin_of[lag_phase], zero)], axis=2
    )
    first_lag = np.arange(tm) * (2 * LAG // tm) - LAG
    turn_angle = 2.0 * np.pi / length * (freq.reshape(1, -1) * first_lag[:, None] % length)
    cosine, sine = np.cos(turn_angle), np.sin(turn_angle)
    turn = np.stack([np.stack([cosine, cosine], axis=2), np.stack([-sine, sine], axis=2)], axis=1)
    turn = np.repeat(turn.astype(np.float32), 64, axis=3)
    return forward.astype(ml_dtypes.bfloat16), lag.astype(ml_dtypes.bfloat16), turn


def kernel(
    blocks, tm,
    x_hbm, hann_hbm, slot_hbm, pairs_hbm, tab_hbm, lag_hbm, turn_hbm, out,
    x, hann, slot_row, pairs, tab, lag, slot_col, ends, folded, water, spec_out, spec_in, water_in, ends_in, onehot, white,
    part_out, part_in, pack_out, pack_in, turn, total_out,
    local_sem, x_sem, tab_sem, ends_s, ends_r, spec_s, spec_r, water_s, water_r,
    part_s, part_r, pack_s, pack_r, last_s, last_r,
):
    me, mine = lax.axis_index("pairs"), lax.axis_index("tm")
    def wrapped(base, size):
        return [jnp.where(base + s >= size, base + s - size, base + s) for s in range(size)]

    block_at, tm_at = wrapped(me, blocks), wrapped(mine, tm)
    bins_each, chunks, bins, half = split(blocks, tm)
    chunk = bins_each // chunks
    group = blocks // RADIX
    length = x.shape[1]
    short = length // RADIX
    stations = onehot.shape[1]

    lag_copy = pltpu.make_async_copy(lag_hbm, lag, local_sem.at[0])
    turn_copy = pltpu.make_async_copy(turn_hbm.at[mine], turn, local_sem.at[1])
    hann_copy = pltpu.make_async_copy(hann_hbm, hann, local_sem.at[2])
    slot_copy = pltpu.make_async_copy(slot_hbm, slot_row, local_sem.at[3])
    pairs_copy = pltpu.make_async_copy(pairs_hbm, pairs, local_sem.at[4])

    def x_copy(i):
        at = pl.ds(pl.multiple_of(i * 16, 16), 16)
        return pltpu.make_async_copy(x_hbm.at[at], x.at[at], x_sem.at[i])

    hann_copy.start()
    x_copy(0).start()
    pairs_copy.start()
    slot_copy.start()

    def step_of(i):
        return 1 + (i + blocks // 2 - 1) % (blocks - 1)

    def table_copy(s):
        return pltpu.make_async_copy(tab_hbm.at[block_at[s]], tab.at[s], tab_sem.at[s])

    def on_pairs(device):
        return {"pairs": device}

    def on_tm(device):
        return {"tm": device}

    barrier = pltpu.get_barrier_semaphore()
    for s in range(1, blocks):
        pl.semaphore_signal(barrier, inc=1, device_id=on_pairs(block_at[s]), device_id_type=MESH)
    for s in range(1, tm):
        pl.semaphore_signal(barrier, inc=1, device_id=on_tm(tm_at[s]), device_id_type=MESH)
    for i in range(1, 8):
        x_copy(i).start()
    for i in range(blocks - 1):
        table_copy(step_of(i)).start()
    table_copy(0).start()

    def remote(src, dst, send, recv, device):
        return pltpu.make_async_remote_copy(
            src_ref=src, dst_ref=dst, send_sem=send, recv_sem=recv, device_id=device, device_id_type=MESH
        )

    def ends_copy(s):
        return remote(ends, ends_in.at[me], ends_s.at[s], ends_r.at[s], on_pairs(block_at[s]))

    def spec_copy(c, s):
        to = on_pairs(block_at[s])
        return remote(spec_out.at[c, s], spec_in.at[c, me], spec_s.at[c, s], spec_r.at[c, s], to)

    def water_copy(s):
        return remote(water, water_in.at[me], water_s.at[s], water_r.at[s], on_pairs(block_at[s]))

    def part_copy(c, s):
        to = tm_at[s]
        return remote(part_out.at[c, to], part_in.at[c, mine], part_s.at[c, s], part_r.at[c, s], on_tm(to))

    def pack_copy(c, s):
        to = block_at[s]
        return remote(pack_out.at[c, to], pack_in.at[c, mine, me], pack_s.at[c, s], pack_r.at[c, s], on_pairs(to))

    def last_copy(c, s):
        to = on_tm(tm_at[s])
        return remote(pack_in.at[c, mine], pack_in.at[c, mine], last_s.at[c, s], last_r.at[c, s], to)

    def each(low, high, act):
        for s in range(low, high):
            act(s)

    hann_copy.wait()
    root = math.sqrt(0.5)

    def fold(i, c):
        low = pl.ds(pl.multiple_of(i * 16, 16), 16)
        high = pl.ds(pl.multiple_of(128 + i * 16, 16), 16)
        x_copy(i).wait()
        mean = jnp.sum(x[low, :], axis=1, keepdims=True) * (1.0 / length)
        for k in range(short // 128):
            v = []
            for q in range(RADIX):
                cols = slice(q * short + k * 128, q * short + (k + 1) * 128)
                v.append((x[low, cols] - mean) * hann[q:q + 1, k * 128:(k + 1) * 128])
            u = [v[q] + v[q + 4] for q in range(4)]
            d = [v[q] - v[q + 4] for q in range(4)]
            dm, dp = root * (d[1] - d[3]), root * (d[1] + d[3])
            even, odd = u[0] + u[2], u[1] + u[3]
            a2, b2 = u[0] - u[2], u[3] - u[1]
            a1, b1 = d[0] + dm, -d[2] - dp
            a3, b3 = d[0] - dm, d[2] - dp
            zero = jnp.zeros_like(even)
            classes = [
                (even + odd, zero), (a1, b1), (a2, b2), (a3, b3),
                (even - odd, zero), (a3, -b3), (a2, -b2), (a1, -b1),
            ]
            cols = slice(k * 128, (k + 1) * 128)
            for r, (a, b) in enumerate(classes):
                folded[r, low, cols] = a.astype(BF16)
                folded[r, high, cols] = b.astype(BF16)
        return c

    lax.fori_loop(0, 8, fold, 0)
    water[...] = jnp.zeros_like(water)

    pl.semaphore_wait(barrier, blocks + tm - 2)
    pairs_copy.wait()
    ends[...] = jnp.zeros_like(ends)
    ends[0:1, 0:64] = pairs[0:1, :].astype(F32)
    ends[0:1, 64:128] = pairs[1:2, :].astype(F32)
    each(1, blocks, lambda s: ends_copy(s).start())
    ends_in[me] = ends[...]

    def spectrum(s):
        table_copy(s).wait()
        to = block_at[s]
        product = lax.dot_general(
            tab[s], folded[to // group], (((1,), (1,)), ((), ())), preferred_element_type=F32
        )
        re = product[:bins_each, :128] + product[bins_each:, 128:]
        im = product[:bins_each, 128:] - product[bins_each:, :128]
        water[...] += jnp.broadcast_to(jnp.sum(re * re + im * im, axis=0, keepdims=True), water.shape)
        return re.astype(BF16), im.astype(BF16)

    def send_block(s):
        re, im = spectrum(s)
        for part in range(chunks):
            spec_out[part, s, :chunk] = re[part * chunk:(part + 1) * chunk]
            spec_out[part, s, chunk:] = im[part * chunk:(part + 1) * chunk]
        spec_copy(0, s).start()

    for i in range(blocks - 1):
        send_block(step_of(i))
    re, im = spectrum(0)
    for part in range(chunks):
        spec_in[part, me, :chunk] = re[part * chunk:(part + 1) * chunk]
        spec_in[part, me, chunk:] = im[part * chunk:(part + 1) * chunk]
    water_in[me] = water[...]
    each(1, blocks, lambda s: water_copy(s).start())

    order = [step_of(i) for i in range(blocks - 1)]
    for part in range(1, min(chunks, 2)):
        for s in order:
            spec_copy(part, s).start()

    slot_copy.wait()
    for k in range(stations // 128):
        cols = slice(k * 128, (k + 1) * 128)
        slot_col[cols, :] = jnp.broadcast_to(slot_row[0:1, cols].astype(F32), (128, 128)).T
    lane = lax.broadcasted_iota(jnp.int32, (1, 128), 1)
    row_ids = lax.broadcasted_iota(jnp.int32, (stations, 256), 0).astype(F32)
    each(1, blocks, lambda s: ends_copy(s).wait())

    def swap(v):
        return pltpu.roll(v, 64, 1)

    def pick(g, c):
        a, b = ends_in[2 * g], ends_in[2 * g + 1]
        left = jnp.where(lane < 64, a, swap(b))[0:1]
        right = jnp.where(lane < 64, swap(a), b)[0:1]
        names = jnp.concatenate([left, right], axis=1)
        slots = jnp.concatenate([slot_col[...], slot_col[...]], axis=1)
        slots = jnp.sum(jnp.where(row_ids == names, slots, 0.0), axis=0, keepdims=True)
        onehot[g] = jnp.where(row_ids == slots, 1.0, 0.0).astype(BF16)
        return c

    lax.fori_loop(0, blocks // 2, pick, 0, unroll=2)

    if half > bins:
        part_out[...] = jnp.zeros_like(part_out)

    def cross_chunk(part):
        def whiten(src):
            re = spec_in[part, src, :chunk].astype(F32)
            im = spec_in[part, src, chunk:].astype(F32)
            level = water_in[src][0:1] * (0.1 / F) + 1e-6
            factor = lax.rsqrt(re * re + im * im + level)
            return re * factor, im * factor

        def whiten_two(q, c):
            cols = pl.ds(pl.multiple_of(q * 128, 128), 128)
            one, two = whiten(2 * q), whiten(2 * q + 1)
            for k in range(2):
                first = jnp.where(lane < 64, one[k], swap(two[k]))
                second = jnp.where(lane < 64, swap(one[k]), two[k])
                at = k * chunk
                white[at:at + chunk, cols] = first.astype(BF16)
                at += 2 * chunk
                white[at:at + chunk, cols] = second.astype(BF16)
            return c

        lax.fori_loop(0, blocks // 2, whiten_two, 0, unroll=2)

        def cross(g, c):
            got = jnp.dot(white[...], onehot[g], preferred_element_type=F32)
            real = imag = None
            for w in range(2):
                at = 2 * w * chunk
                lr, rr = got[at:at + chunk, :128], got[at:at + chunk, 128:]
                at += chunk
                li, ri = got[at:at + chunk, :128], got[at:at + chunk, 128:]
                re, im = lr * rr + li * ri, li * rr - lr * ri
                real = re if real is None else real + re
                imag = im if imag is None else imag + im
            for t in range(tm):
                rows = slice(t * bins, (t + 1) * bins)
                part_out[part, t, g, :bins] = real[rows].astype(BF16)
                part_out[part, t, g, half:half + bins] = imag[rows].astype(BF16)
            return c

        lax.fori_loop(0, blocks // 2, cross, 0, unroll=4)
        each(1, tm, lambda s: part_copy(part, s).start())
        part_in[part, mine] = part_out[part, mine]

    def pack_chunk(part):
        each(1, tm, lambda s: part_copy(part, s).wait())

        def pack(g, c):
            total = part_in[part, 0, g].astype(F32)
            for t in range(1, tm):
                total += part_in[part, t, g].astype(F32)
            top, bottom = total[:half], total[half:]
            pack_out[part, 2 * g] = jnp.where(lane < 64, top, swap(bottom)).astype(BF16)
            pack_out[part, 2 * g + 1] = jnp.where(lane < 64, swap(top), bottom).astype(BF16)
            return c

        lax.fori_loop(0, blocks // 2, pack, 0, unroll=4)
        each(1, blocks, lambda s: pack_copy(part, s).start())
        pack_in[part, mine, me] = pack_out[part, me]

    def share_chunk(part):
        each(1, blocks, lambda s: pack_copy(part, s).wait())
        each(1, tm, lambda s: last_copy(part, s).start())

    def lag_chunk(part):
        each(1, tm, lambda s: last_copy(part, s).wait())
        count = tm * blocks * half
        at = slice(part * count, (part + 1) * count)
        stacked = pack_in[part].reshape(count, 128).astype(F32)
        turned = stacked * turn[0, at, :] + swap(stacked) * turn[1, at, :]
        values = jnp.concatenate([turned, swap(turned)], axis=0).astype(BF16)
        product = jnp.dot(lag[part], values, preferred_element_type=F32)
        total_out[...] = product if part == 0 else total_out[...] + product

    lag_copy.start()
    turn_copy.start()
    for part in range(2, chunks):
        for s in order:
            spec_copy(part - 2, s).wait_send()
            spec_copy(part, s).start()
    each(1, blocks, lambda s: water_copy(s).wait_recv())
    for part in range(chunks):
        each(1, blocks, lambda s: spec_copy(part, s).wait_recv())
        cross_chunk(part)
        if 0 < part < chunks - 1:
            share_chunk(part - 1)
        pack_chunk(part)
    lag_copy.wait()
    turn_copy.wait()
    if chunks > 1:
        share_chunk(chunks - 2)
    for part in range(chunks - 2):
        lag_chunk(part)
    share_chunk(chunks - 1)
    for part in range(max(0, chunks - 2), chunks):
        lag_chunk(part)
    for part in range(max(0, chunks - 2), chunks):
        for s in order:
            spec_copy(part, s).wait_send()
    each(1, blocks, lambda s: water_copy(s).wait_send())
    out[...] = total_out[...].T[:64]


def on_device(traces, station_slot, pair_stations):
    held, stations_each, length = traces.shape
    stations = station_slot.shape[0]
    blocks, tm = lax.axis_size("pairs"), lax.axis_size("tm")
    pairs_each = pair_stations.shape[0]
    assert held * stations_each == 128 and held == 2 and pairs_each == 64 and blocks % RADIX == 0
    bins_each, chunks, bins, half = split(blocks, tm)
    short = length // RADIX
    values = tm * blocks * half
    lag_rows = 2 * LAG // tm
    forward, lag, turn = tables(length, blocks, tm)
    times = (np.arange(length, dtype=np.float64) + 0.5) * (2.0 * np.pi / length)
    hann = (0.5 - 0.5 * np.cos(times)).astype(np.float32).reshape(RADIX, short)
    scale = 1.0 / math.sqrt(F * held * tm)
    vmem = pl.BlockSpec(memory_space=pltpu.VMEM)
    anywhere = pl.BlockSpec(memory_space=pl.ANY)
    dma = pltpu.SemaphoreType.DMA
    result = pl.pallas_call(
        functools.partial(kernel, blocks, tm),
        out_shape=jax.ShapeDtypeStruct((pairs_each, lag_rows), F32),
        in_specs=[anywhere, anywhere, anywhere, anywhere, anywhere, anywhere, anywhere],
        out_specs=vmem,
        scratch_shapes=[
            pltpu.VMEM((128, length), F32),
            pltpu.VMEM((RADIX, short), F32),
            pltpu.VMEM((1, stations), jnp.int32),
            pltpu.VMEM((2, pairs_each), jnp.int32),
            pltpu.VMEM((blocks, 2 * bins_each, short), BF16),
            pltpu.VMEM((chunks, lag_rows, 2 * values), BF16),
            pltpu.VMEM((stations, 128), F32),
            pltpu.VMEM((8, 128), F32),
            pltpu.VMEM((RADIX, 256, short), BF16),
            pltpu.VMEM((8, 128), F32),
            pltpu.VMEM((chunks, blocks, 2 * bins_each // chunks, 128), BF16),
            pltpu.VMEM((chunks, blocks, 2 * bins_each // chunks, 128), BF16),
            pltpu.VMEM((blocks, 8, 128), F32),
            pltpu.VMEM((blocks, 8, 128), F32),
            pltpu.VMEM((blocks // 2, stations, 256), BF16),
            pltpu.VMEM((4 * bins_each // chunks, stations), BF16),
            pltpu.VMEM((chunks, tm, blocks // 2, 2 * half, 128), BF16),
            pltpu.VMEM((chunks, tm, blocks // 2, 2 * half, 128), BF16),
            pltpu.VMEM((chunks, blocks, half, 128), BF16),
            pltpu.VMEM((chunks, tm, blocks, half, 128), BF16),
            pltpu.VMEM((2, chunks * values, 128), F32),
            pltpu.VMEM((lag_rows, 128), F32),
            dma((5,)), dma((8,)), dma((blocks,)),
            dma((blocks,)), dma((blocks,)),
            dma((chunks, blocks)), dma((chunks, blocks)),
            dma((blocks,)), dma((blocks,)),
            dma((chunks, tm)), dma((chunks, tm)),
            dma((chunks, blocks)), dma((chunks, blocks)),
            dma((chunks, tm)), dma((chunks, tm)),
        ],
        compiler_params=pltpu.CompilerParams(
            collective_id=0, has_side_effects=True, vmem_limit_bytes=56 * 1024 * 1024
        ),
    )(
        traces.reshape(128, length), jnp.asarray(hann), station_slot.reshape(1, stations),
        pair_stations.T, jnp.asarray(forward), jnp.asarray(lag), jnp.asarray(turn),
    )
    return result.T * scale


def solution(mesh):
    in_specs = (P("tm", "pairs", None), P(), P("pairs", None))
    out_specs = P("tm", "pairs")
    return jax.shard_map(
        on_device, mesh=mesh, in_specs=in_specs, out_specs=out_specs, check_vma=False
    )
```

```python
import functools
import math

import jax
import jax.numpy as jnp
import ml_dtypes
import numpy as np
from jax import lax
from jax.experimental import pallas as pl
from jax.experimental.pallas import tpu as pltpu
from jax.sharding import PartitionSpec as P

F = 1536
FLO = 32
LAG = 1024
RADIX = 8
MESH = pl.DeviceIdType.MESH
F32 = jnp.float32
BF16 = jnp.bfloat16


def split(blocks, tm):
    bins_each = F // blocks
    chunks = 1
    bins = bins_each // (chunks * tm)
    return bins_each, chunks, bins, -(-bins // 16) * 16


def tables(length, blocks, tm):
    bins_each, chunks, bins, half = split(blocks, tm)
    group = blocks // RADIX
    short = length // RADIX
    angles = 2.0 * np.pi * np.arange(length) / length
    cos_of = np.cos(angles).astype(np.float32).astype(ml_dtypes.bfloat16)
    sin_of = np.sin(angles).astype(np.float32).astype(ml_dtypes.bfloat16)
    block_ids = np.arange(blocks)
    first = block_ids // group + RADIX * (block_ids % group) * bins_each
    freqs = FLO + first[:, None] + RADIX * np.arange(bins_each)[None, :]
    phases = freqs[:, :, None] * np.arange(short)[None, None, :] % length
    forward = np.concatenate([cos_of[phases], sin_of[phases]], axis=1)

    inside = np.arange(half)
    value = np.arange(chunks * tm)[:, None] * bins + np.minimum(inside, bins - 1)[None, :]
    freq = freqs[block_ids[None, :, None], value[:, None, :]].reshape(chunks, 1, -1)
    valid = np.broadcast_to(inside < bins, (chunks, tm, blocks, half)).reshape(chunks, 1, -1)
    lag_phase = freq * np.arange(2 * LAG // tm)[None, :, None] % length
    zero = np.zeros((), ml_dtypes.bfloat16)
    lag = np.concatenate(
        [np.where(valid, cos_of[lag_phase], zero), np.where(valid, -sin_of[lag_phase], zero)], axis=2
    )
    first_lag = np.arange(tm) * (2 * LAG // tm) - LAG
    turn_angle = 2.0 * np.pi / length * (freq.reshape(1, -1) * first_lag[:, None] % length)
    cosine, sine = np.cos(turn_angle), np.sin(turn_angle)
    turn = np.stack([np.stack([cosine, cosine], axis=2), np.stack([-sine, sine], axis=2)], axis=1)
    turn = np.repeat(turn.astype(np.float32), 64, axis=3)
    return forward.astype(ml_dtypes.bfloat16), lag.astype(ml_dtypes.bfloat16), turn


def kernel(
    blocks, tm,
    x_hbm, hann_hbm, slot_hbm, pairs_hbm, tab_hbm, lag_hbm, turn_hbm, out,
    x, hann, slot_row, pairs, tab, lag, slot_col, ends, folded, water, spec_out, spec_in, water_in, ends_in, onehot, white,
    part_out, part_in, pack_out, pack_in, turn, total_out,
    local_sem, x_sem, tab_sem, ends_s, ends_r, spec_s, spec_r, water_s, water_r,
    part_s, part_r, pack_s, pack_r, last_s, last_r,
):
    me, mine = lax.axis_index("pairs"), lax.axis_index("tm")
    def wrapped(base, size):
        return [jnp.where(base + s >= size, base + s - size, base + s) for s in range(size)]

    block_at, tm_at = wrapped(me, blocks), wrapped(mine, tm)
    bins_each, chunks, bins, half = split(blocks, tm)
    chunk = bins_each // chunks
    group = blocks // RADIX
    length = x.shape[1]
    short = length // RADIX
    stations = onehot.shape[1]

    lag_copy = pltpu.make_async_copy(lag_hbm, lag, local_sem.at[0])
    turn_copy = pltpu.make_async_copy(turn_hbm.at[mine], turn, local_sem.at[1])
    hann_copy = pltpu.make_async_copy(hann_hbm, hann, local_sem.at[2])
    slot_copy = pltpu.make_async_copy(slot_hbm, slot_row, local_sem.at[3])
    pairs_copy = pltpu.make_async_copy(pairs_hbm, pairs, local_sem.at[4])

    def x_copy(i):
        at = pl.ds(pl.multiple_of(i * 16, 16), 16)
        return pltpu.make_async_copy(x_hbm.at[at], x.at[at], x_sem.at[i])

    hann_copy.start()
    x_copy(0).start()
    pairs_copy.start()
    slot_copy.start()

    def step_of(i):
        return 1 + (i + blocks // 2 - 1) % (blocks - 1)

    def table_copy(s):
        return pltpu.make_async_copy(tab_hbm.at[block_at[s]], tab.at[s], tab_sem.at[s])

    def on_pairs(device):
        return {"pairs": device}

    def on_tm(device):
        return {"tm": device}

    barrier = pltpu.get_barrier_semaphore()
    for s in range(1, blocks):
        pl.semaphore_signal(barrier, inc=1, device_id=on_pairs(block_at[s]), device_id_type=MESH)
    for s in range(1, tm):
        pl.semaphore_signal(barrier, inc=1, device_id=on_tm(tm_at[s]), device_id_type=MESH)
    for i in range(1, 8):
        x_copy(i).start()
    for i in range(blocks - 1):
        table_copy(step_of(i)).start()
    table_copy(0).start()

    def remote(src, dst, send, recv, device):
        return pltpu.make_async_remote_copy(
            src_ref=src, dst_ref=dst, send_sem=send, recv_sem=recv, device_id=device, device_id_type=MESH
        )

    def ends_copy(s):
        return remote(ends, ends_in.at[me], ends_s.at[s], ends_r.at[s], on_pairs(block_at[s]))

    def spec_copy(c, s):
        to = on_pairs(block_at[s])
        return remote(spec_out.at[c, s], spec_in.at[c, me], spec_s.at[c, s], spec_r.at[c, s], to)

    def water_copy(s):
        return remote(water, water_in.at[me], water_s.at[s], water_r.at[s], on_pairs(block_at[s]))

    def part_copy(c, s):
        to = tm_at[s]
        return remote(part_out.at[c, to], part_in.at[c, mine], part_s.at[c, s], part_r.at[c, s], on_tm(to))

    def pack_copy(c, s):
        to = block_at[s]
        return remote(pack_out.at[c, to], pack_in.at[c, mine, me], pack_s.at[c, s], pack_r.at[c, s], on_pairs(to))

    def last_copy(c, s):
        to = on_tm(tm_at[s])
        return remote(pack_in.at[c, mine], pack_in.at[c, mine], last_s.at[c, s], last_r.at[c, s], to)

    def each(low, high, act):
        for s in range(low, high):
            act(s)

    for r in (0, RADIX // 2):
        folded[r, 128:, :] = jnp.zeros((128, short), BF16)
    hann_copy.wait()
    root = math.sqrt(0.5)

    def fold(i, c):
        low = pl.ds(pl.multiple_of(i * 16, 16), 16)
        high = pl.ds(pl.multiple_of(128 + i * 16, 16), 16)
        x_copy(i).wait()
        mean = jnp.sum(x[low, :], axis=1, keepdims=True) * (1.0 / length)
        for k in range(short // 128):
            v = []
            for q in range(RADIX):
                cols = slice(q * short + k * 128, q * short + (k + 1) * 128)
                v.append((x[low, cols] - mean) * hann[q:q + 1, k * 128:(k + 1) * 128])
            u = [v[q] + v[q + 4] for q in range(4)]
            d = [v[q] - v[q + 4] for q in range(4)]
            dm, dp = root * (d[1] - d[3]), root * (d[1] + d[3])
            even, odd = u[0] + u[2], u[1] + u[3]
            a2, b2 = u[0] - u[2], u[3] - u[1]
            a1, b1 = d[0] + dm, -d[2] - dp
            a3, b3 = d[0] - dm, d[2] - dp
            classes = [
                (even + odd, None), (a1, b1), (a2, b2), (a3, b3),
                (even - odd, None), (a3, -b3), (a2, -b2), (a1, -b1),
            ]
            cols = slice(k * 128, (k + 1) * 128)
            for r, (a, b) in enumerate(classes):
                folded[r, low, cols] = a.astype(BF16)
                if b is not None:
                    folded[r, high, cols] = b.astype(BF16)
        return c

    lax.fori_loop(0, 8, fold, 0)
    water[...] = jnp.zeros_like(water)

    pl.semaphore_wait(barrier, blocks + tm - 2)
    pairs_copy.wait()
    ends[...] = jnp.zeros_like(ends)
    ends[0:1, 0:64] = pairs[0:1, :].astype(F32)
    ends[0:1, 64:128] = pairs[1:2, :].astype(F32)
    each(1, blocks, lambda s: ends_copy(s).start())
    ends_in[me] = ends[...]

    def spectrum(s):
        table_copy(s).wait()
        to = block_at[s]
        product = lax.dot_general(
            tab[s], folded[to // group], (((1,), (1,)), ((), ())), preferred_element_type=F32
        )
        re = product[:bins_each, :128] + product[bins_each:, 128:]
        im = product[:bins_each, 128:] - product[bins_each:, :128]
        water[...] += jnp.broadcast_to(jnp.sum(re * re + im * im, axis=0, keepdims=True), water.shape)
        return re.astype(BF16), im.astype(BF16)

    def send_block(s):
        re, im = spectrum(s)
        for part in range(chunks):
            spec_out[part, s, :chunk] = re[part * chunk:(part + 1) * chunk]
            spec_out[part, s, chunk:] = im[part * chunk:(part + 1) * chunk]
        spec_copy(0, s).start()

    for i in range(blocks - 1):
        send_block(step_of(i))
    re, im = spectrum(0)
    for part in range(chunks):
        spec_in[part, me, :chunk] = re[part * chunk:(part + 1) * chunk]
        spec_in[part, me, chunk:] = im[part * chunk:(part + 1) * chunk]
    water_in[me] = water[...]
    each(1, blocks, lambda s: water_copy(s).start())

    order = [step_of(i) for i in range(blocks - 1)]
    for part in range(1, min(chunks, 2)):
        for s in order:
            spec_copy(part, s).start()

    slot_copy.wait()
    for k in range(stations // 128):
        cols = slice(k * 128, (k + 1) * 128)
        slot_col[cols, :] = jnp.broadcast_to(slot_row[0:1, cols].astype(F32), (128, 128)).T
    lane = lax.broadcasted_iota(jnp.int32, (1, 128), 1)
    row_ids = lax.broadcasted_iota(jnp.int32, (stations, 256), 0).astype(F32)
    each(1, blocks, lambda s: ends_copy(s).wait())

    def swap(v):
        return pltpu.roll(v, 64, 1)

    def pick(g, c):
        a, b = ends_in[2 * g], ends_in[2 * g + 1]
        left = jnp.where(lane < 64, a, swap(b))[0:1]
        right = jnp.where(lane < 64, swap(a), b)[0:1]
        names = jnp.concatenate([left, right], axis=1)
        slots = jnp.concatenate([slot_col[...], slot_col[...]], axis=1)
        slots = jnp.sum(jnp.where(row_ids == names, slots, 0.0), axis=0, keepdims=True)
        onehot[g] = jnp.where(row_ids == slots, 1.0, 0.0).astype(BF16)
        return c

    lax.fori_loop(0, blocks // 2, pick, 0, unroll=2)

    if half > bins:
        part_out[...] = jnp.zeros_like(part_out)

    def cross_chunk(part):
        def whiten(src):
            re = spec_in[part, src, :chunk].astype(F32)
            im = spec_in[part, src, chunk:].astype(F32)
            level = water_in[src][0:1] * (0.1 / F) + 1e-6
            factor = lax.rsqrt(re * re + im * im + level)
            return re * factor, im * factor

        def whiten_two(q, c):
            cols = pl.ds(pl.multiple_of(q * 128, 128), 128)
            one, two = whiten(2 * q), whiten(2 * q + 1)
            for k in range(2):
                first = jnp.where(lane < 64, one[k], swap(two[k]))
                second = jnp.where(lane < 64, swap(one[k]), two[k])
                at = k * chunk
                white[at:at + chunk, cols] = first.astype(BF16)
                at += 2 * chunk
                white[at:at + chunk, cols] = second.astype(BF16)
            return c

        lax.fori_loop(0, blocks // 2, whiten_two, 0, unroll=2)

        def cross(g, c):
            got = jnp.dot(white[...], onehot[g], preferred_element_type=F32)
            real = imag = None
            for w in range(2):
                at = 2 * w * chunk
                lr, rr = got[at:at + chunk, :128], got[at:at + chunk, 128:]
                at += chunk
                li, ri = got[at:at + chunk, :128], got[at:at + chunk, 128:]
                re, im = lr * rr + li * ri, li * rr - lr * ri
                real = re if real is None else real + re
                imag = im if imag is None else imag + im
            for t in range(tm):
                rows = slice(t * bins, (t + 1) * bins)
                part_out[part, t, g, :bins] = real[rows].astype(BF16)
                part_out[part, t, g, half:half + bins] = imag[rows].astype(BF16)
            return c

        lax.fori_loop(0, blocks // 2, cross, 0, unroll=4)
        each(1, tm, lambda s: part_copy(part, s).start())
        part_in[part, mine] = part_out[part, mine]

    def pack_chunk(part):
        each(1, tm, lambda s: part_copy(part, s).wait())

        def pack(g, c):
            total = part_in[part, 0, g].astype(F32)
            for t in range(1, tm):
                total += part_in[part, t, g].astype(F32)
            top, bottom = total[:half], total[half:]
            pack_out[part, 2 * g] = jnp.where(lane < 64, top, swap(bottom)).astype(BF16)
            pack_out[part, 2 * g + 1] = jnp.where(lane < 64, swap(top), bottom).astype(BF16)
            return c

        lax.fori_loop(0, blocks // 2, pack, 0, unroll=4)
        each(1, blocks, lambda s: pack_copy(part, s).start())
        pack_in[part, mine, me] = pack_out[part, me]

    def share_chunk(part):
        each(1, blocks, lambda s: pack_copy(part, s).wait())
        each(1, tm, lambda s: last_copy(part, s).start())

    def lag_chunk(part):
        each(1, tm, lambda s: last_copy(part, s).wait())
        count = tm * blocks * half
        at = slice(part * count, (part + 1) * count)
        stacked = pack_in[part].reshape(count, 128).astype(F32)
        turned = stacked * turn[0, at, :] + swap(stacked) * turn[1, at, :]
        values = jnp.concatenate([turned, swap(turned)], axis=0).astype(BF16)
        product = jnp.dot(lag[part], values, preferred_element_type=F32)
        total_out[...] = product if part == 0 else total_out[...] + product

    lag_copy.start()
    turn_copy.start()
    for part in range(2, chunks):
        for s in order:
            spec_copy(part - 2, s).wait_send()
            spec_copy(part, s).start()
    each(1, blocks, lambda s: water_copy(s).wait_recv())
    for part in range(chunks):
        each(1, blocks, lambda s: spec_copy(part, s).wait_recv())
        cross_chunk(part)
        if 0 < part < chunks - 1:
            share_chunk(part - 1)
        pack_chunk(part)
    lag_copy.wait()
    turn_copy.wait()
    if chunks > 1:
        share_chunk(chunks - 2)
    for part in range(chunks - 2):
        lag_chunk(part)
    share_chunk(chunks - 1)
    for part in range(max(0, chunks - 2), chunks):
        lag_chunk(part)
    for part in range(max(0, chunks - 2), chunks):
        for s in order:
            spec_copy(part, s).wait_send()
    each(1, blocks, lambda s: water_copy(s).wait_send())
    out[...] = total_out[...].T[:64]


def on_device(traces, station_slot, pair_stations):
    held, stations_each, length = traces.shape
    stations = station_slot.shape[0]
    blocks, tm = lax.axis_size("pairs"), lax.axis_size("tm")
    pairs_each = pair_stations.shape[0]
    assert held * stations_each == 128 and held == 2 and pairs_each == 64 and blocks % RADIX == 0
    bins_each, chunks, bins, half = split(blocks, tm)
    short = length // RADIX
    values = tm * blocks * half
    lag_rows = 2 * LAG // tm
    forward, lag, turn = tables(length, blocks, tm)
    times = (np.arange(length, dtype=np.float64) + 0.5) * (2.0 * np.pi / length)
    hann = (0.5 - 0.5 * np.cos(times)).astype(np.float32).reshape(RADIX, short)
    scale = 1.0 / math.sqrt(F * held * tm)
    vmem = pl.BlockSpec(memory_space=pltpu.VMEM)
    anywhere = pl.BlockSpec(memory_space=pl.ANY)
    dma = pltpu.SemaphoreType.DMA
    result = pl.pallas_call(
        functools.partial(kernel, blocks, tm),
        out_shape=jax.ShapeDtypeStruct((pairs_each, lag_rows), F32),
        in_specs=[anywhere, anywhere, anywhere, anywhere, anywhere, anywhere, anywhere],
        out_specs=vmem,
        scratch_shapes=[
            pltpu.VMEM((128, length), F32),
            pltpu.VMEM((RADIX, short), F32),
            pltpu.VMEM((1, stations), jnp.int32),
            pltpu.VMEM((2, pairs_each), jnp.int32),
            pltpu.VMEM((blocks, 2 * bins_each, short), BF16),
            pltpu.VMEM((chunks, lag_rows, 2 * values), BF16),
            pltpu.VMEM((stations, 128), F32),
            pltpu.VMEM((8, 128), F32),
            pltpu.VMEM((RADIX, 256, short), BF16),
            pltpu.VMEM((8, 128), F32),
            pltpu.VMEM((chunks, blocks, 2 * bins_each // chunks, 128), BF16),
            pltpu.VMEM((chunks, blocks, 2 * bins_each // chunks, 128), BF16),
            pltpu.VMEM((blocks, 8, 128), F32),
            pltpu.VMEM((blocks, 8, 128), F32),
            pltpu.VMEM((blocks // 2, stations, 256), BF16),
            pltpu.VMEM((4 * bins_each // chunks, stations), BF16),
            pltpu.VMEM((chunks, tm, blocks // 2, 2 * half, 128), BF16),
            pltpu.VMEM((chunks, tm, blocks // 2, 2 * half, 128), BF16),
            pltpu.VMEM((chunks, blocks, half, 128), BF16),
            pltpu.VMEM((chunks, tm, blocks, half, 128), BF16),
            pltpu.VMEM((2, chunks * values, 128), F32),
            pltpu.VMEM((lag_rows, 128), F32),
            dma((5,)), dma((8,)), dma((blocks,)),
            dma((blocks,)), dma((blocks,)),
            dma((chunks, blocks)), dma((chunks, blocks)),
            dma((blocks,)), dma((blocks,)),
            dma((chunks, tm)), dma((chunks, tm)),
            dma((chunks, blocks)), dma((chunks, blocks)),
            dma((chunks, tm)), dma((chunks, tm)),
        ],
        compiler_params=pltpu.CompilerParams(
            collective_id=0, has_side_effects=True, vmem_limit_bytes=56 * 1024 * 1024
        ),
    )(
        traces.reshape(128, length), jnp.asarray(hann), station_slot.reshape(1, stations),
        pair_stations.T, jnp.asarray(forward), jnp.asarray(lag), jnp.asarray(turn),
    )
    return result.T * scale


def solution(mesh):
    in_specs = (P("tm", "pairs", None), P(), P("pairs", None))
    out_specs = P("tm", "pairs")
    return jax.shard_map(
        on_device, mesh=mesh, in_specs=in_specs, out_specs=out_specs, check_vma=False
    )
```

```python
import functools
import math

import jax
import jax.numpy as jnp
import ml_dtypes
import numpy as np
from jax import lax
from jax.experimental import pallas as pl
from jax.experimental.pallas import tpu as pltpu
from jax.sharding import PartitionSpec as P

F = 1536
FLO = 32
LAG = 1024
RADIX = 8
MESH = pl.DeviceIdType.MESH
F32 = jnp.float32
BF16 = jnp.bfloat16


def split(blocks, tm):
    bins_each = F // blocks
    chunks = max(1, bins_each // (16 * tm))
    while bins_each % (chunks * tm):
        chunks -= 1
    bins = bins_each // (chunks * tm)
    return bins_each, chunks, bins, -(-bins // 16) * 16


def tables(length, blocks, tm):
    bins_each, chunks, bins, half = split(blocks, tm)
    group = blocks // RADIX
    short = length // RADIX
    angles = 2.0 * np.pi * np.arange(length) / length
    cos_of = np.cos(angles).astype(np.float32).astype(ml_dtypes.bfloat16)
    sin_of = np.sin(angles).astype(np.float32).astype(ml_dtypes.bfloat16)
    block_ids = np.arange(blocks)
    first = block_ids // group + RADIX * (block_ids % group) * bins_each
    freqs = FLO + first[:, None] + RADIX * np.arange(bins_each)[None, :]
    phases = freqs[:, :, None] * np.arange(short)[None, None, :] % length
    forward = np.concatenate([cos_of[phases], sin_of[phases]], axis=1)

    inside = np.arange(half)
    value = np.arange(chunks * tm)[:, None] * bins + np.minimum(inside, bins - 1)[None, :]
    freq = freqs[block_ids[None, :, None], value[:, None, :]].reshape(chunks, 1, -1)
    valid = np.broadcast_to(inside < bins, (chunks, tm, blocks, half)).reshape(chunks, 1, -1)
    lag_phase = freq * np.arange(2 * LAG // tm)[None, :, None] % length
    zero = np.zeros((), ml_dtypes.bfloat16)
    lag = np.concatenate(
        [np.where(valid, cos_of[lag_phase], zero), np.where(valid, -sin_of[lag_phase], zero)], axis=2
    )
    first_lag = np.arange(tm) * (2 * LAG // tm) - LAG
    turn_angle = 2.0 * np.pi / length * (freq.reshape(1, -1) * first_lag[:, None] % length)
    cosine, sine = np.cos(turn_angle), np.sin(turn_angle)
    turn = np.stack([np.stack([cosine, cosine], axis=2), np.stack([-sine, sine], axis=2)], axis=1)
    turn = np.repeat(turn.astype(np.float32), 64, axis=3)
    return forward.astype(ml_dtypes.bfloat16), lag.astype(ml_dtypes.bfloat16), turn


def kernel(
    blocks, tm,
    x_hbm, hann_hbm, slot_hbm, pairs_hbm, tab_hbm, lag_hbm, turn_hbm, out,
    x, means, hann, slot_row, pairs, tab, lag, slot_col, ends, folded, water, spec_out, spec_in, water_in, ends_in, onehot, white,
    part_out, part_in, pack_out, pack_in, turn, total_out,
    local_sem, x_sem, tab_sem, ends_s, ends_r, spec_s, spec_r, water_s, water_r,
    part_s, part_r, pack_s, pack_r, last_s, last_r,
):
    me, mine = lax.axis_index("pairs"), lax.axis_index("tm")
    def wrapped(base, size):
        return [jnp.where(base + s >= size, base + s - size, base + s) for s in range(size)]

    block_at, tm_at = wrapped(me, blocks), wrapped(mine, tm)
    bins_each, chunks, bins, half = split(blocks, tm)
    chunk = bins_each // chunks
    group = blocks // RADIX
    length = x.shape[1]
    short = length // RADIX
    stations = onehot.shape[1]

    lag_copy = pltpu.make_async_copy(lag_hbm, lag, local_sem.at[0])
    turn_copy = pltpu.make_async_copy(turn_hbm.at[mine], turn, local_sem.at[1])
    hann_copy = pltpu.make_async_copy(hann_hbm, hann, local_sem.at[2])
    slot_copy = pltpu.make_async_copy(slot_hbm, slot_row, local_sem.at[3])
    pairs_copy = pltpu.make_async_copy(pairs_hbm, pairs, local_sem.at[4])

    def x_copy(i):
        at = pl.ds(pl.multiple_of(i * 16, 16), 16)
        return pltpu.make_async_copy(x_hbm.at[at], x.at[at], x_sem.at[i])

    hann_copy.start()
    x_copy(0).start()
    pairs_copy.start()
    slot_copy.start()

    def step_of(i):
        return 1 + (i + blocks // 2 - 1) % (blocks - 1)

    def table_copy(s):
        return pltpu.make_async_copy(tab_hbm.at[block_at[s]], tab.at[s], tab_sem.at[s])

    def on_pairs(device):
        return {"pairs": device}

    def on_tm(device):
        return {"tm": device}

    barrier = pltpu.get_barrier_semaphore()
    for s in range(1, blocks):
        pl.semaphore_signal(barrier, inc=1, device_id=on_pairs(block_at[s]), device_id_type=MESH)
    for s in range(1, tm):
        pl.semaphore_signal(barrier, inc=1, device_id=on_tm(tm_at[s]), device_id_type=MESH)
    for i in range(1, 8):
        x_copy(i).start()
    for i in range(blocks - 1):
        table_copy(step_of(i)).start()
    table_copy(0).start()

    def remote(src, dst, send, recv, device):
        return pltpu.make_async_remote_copy(
            src_ref=src, dst_ref=dst, send_sem=send, recv_sem=recv, device_id=device, device_id_type=MESH
        )

    def ends_copy(s):
        return remote(ends, ends_in.at[me], ends_s.at[s], ends_r.at[s], on_pairs(block_at[s]))

    def spec_copy(c, s):
        to = on_pairs(block_at[s])
        return remote(spec_out.at[c, s], spec_in.at[c, me], spec_s.at[c, s], spec_r.at[c, s], to)

    def water_copy(s):
        return remote(water, water_in.at[me], water_s.at[s], water_r.at[s], on_pairs(block_at[s]))

    def part_copy(c, s):
        to = tm_at[s]
        return remote(part_out.at[c, to], part_in.at[c, mine], part_s.at[c, s], part_r.at[c, s], on_tm(to))

    def pack_copy(c, s):
        to = block_at[s]
        return remote(pack_out.at[c, to], pack_in.at[c, mine, me], pack_s.at[c, s], pack_r.at[c, s], on_pairs(to))

    def last_copy(c, s):
        to = on_tm(tm_at[s])
        return remote(pack_in.at[c, mine], pack_in.at[c, mine], last_s.at[c, s], last_r.at[c, s], to)

    def each(low, high, act):
        for s in range(low, high):
            act(s)

    for r in (0, RADIX // 2):
        folded[r, 128:, :] = jnp.zeros((128, short), BF16)
    hann_copy.wait()
    for i in range(8):
        x_copy(i).wait()
        at = slice(i * 16, (i + 1) * 16)
        mean = jnp.sum(x[at, :], axis=1, keepdims=True) * (1.0 / length)
        means[at, :] = jnp.broadcast_to(mean, (16, 128))
    root = math.sqrt(0.5)

    def fold(i, c):
        low = pl.ds(pl.multiple_of(i * 16, 16), 16)
        high = pl.ds(pl.multiple_of(128 + i * 16, 16), 16)
        mean = means[low, :]
        for k in range(short // 128):
            v = []
            for q in range(RADIX):
                cols = slice(q * short + k * 128, q * short + (k + 1) * 128)
                v.append((x[low, cols] - mean) * hann[q:q + 1, k * 128:(k + 1) * 128])
            u = [v[q] + v[q + 4] for q in range(4)]
            d = [v[q] - v[q + 4] for q in range(4)]
            dm, dp = root * (d[1] - d[3]), root * (d[1] + d[3])
            even, odd = u[0] + u[2], u[1] + u[3]
            a2, b2 = u[0] - u[2], u[3] - u[1]
            a1, b1 = d[0] + dm, -d[2] - dp
            a3, b3 = d[0] - dm, d[2] - dp
            classes = [
                (even + odd, None), (a1, b1), (a2, b2), (a3, b3),
                (even - odd, None), (a3, -b3), (a2, -b2), (a1, -b1),
            ]
            cols = slice(k * 128, (k + 1) * 128)
            for r, (a, b) in enumerate(classes):
                folded[r, low, cols] = a.astype(BF16)
                if b is not None:
                    folded[r, high, cols] = b.astype(BF16)
        return c

    lax.fori_loop(0, 8, fold, 0, unroll=2)
    water[...] = jnp.zeros_like(water)

    pl.semaphore_wait(barrier, blocks + tm - 2)
    pairs_copy.wait()
    ends[...] = jnp.zeros_like(ends)
    ends[0:1, 0:64] = pairs[0:1, :].astype(F32)
    ends[0:1, 64:128] = pairs[1:2, :].astype(F32)
    each(1, blocks, lambda s: ends_copy(s).start())
    ends_in[me] = ends[...]

    def spectrum(s):
        table_copy(s).wait()
        to = block_at[s]
        product = lax.dot_general(
            tab[s], folded[to // group], (((1,), (1,)), ((), ())), preferred_element_type=F32
        )
        re = product[:bins_each, :128] + product[bins_each:, 128:]
        im = product[:bins_each, 128:] - product[bins_each:, :128]
        water[...] += jnp.broadcast_to(jnp.sum(re * re + im * im, axis=0, keepdims=True), water.shape)
        return re.astype(BF16), im.astype(BF16)

    def send_block(s):
        re, im = spectrum(s)
        for part in range(chunks):
            spec_out[part, s, :chunk] = re[part * chunk:(part + 1) * chunk]
            spec_out[part, s, chunk:] = im[part * chunk:(part + 1) * chunk]
        spec_copy(0, s).start()

    for i in range(blocks - 1):
        send_block(step_of(i))
    re, im = spectrum(0)
    for part in range(chunks):
        spec_in[part, me, :chunk] = re[part * chunk:(part + 1) * chunk]
        spec_in[part, me, chunk:] = im[part * chunk:(part + 1) * chunk]
    water_in[me] = water[...]
    each(1, blocks, lambda s: water_copy(s).start())

    order = [step_of(i) for i in range(blocks - 1)]
    for part in range(1, min(chunks, 2)):
        for s in order:
            spec_copy(part, s).start()

    slot_copy.wait()
    for k in range(stations // 128):
        cols = slice(k * 128, (k + 1) * 128)
        slot_col[cols, :] = jnp.broadcast_to(slot_row[0:1, cols].astype(F32), (128, 128)).T
    lane = lax.broadcasted_iota(jnp.int32, (1, 128), 1)
    row_ids = lax.broadcasted_iota(jnp.int32, (stations, 256), 0).astype(F32)
    each(1, blocks, lambda s: ends_copy(s).wait())

    def swap(v):
        return pltpu.roll(v, 64, 1)

    def pick(g, c):
        a, b = ends_in[2 * g], ends_in[2 * g + 1]
        left = jnp.where(lane < 64, a, swap(b))[0:1]
        right = jnp.where(lane < 64, swap(a), b)[0:1]
        names = jnp.concatenate([left, right], axis=1)
        slots = jnp.concatenate([slot_col[...], slot_col[...]], axis=1)
        slots = jnp.sum(jnp.where(row_ids == names, slots, 0.0), axis=0, keepdims=True)
        onehot[g] = jnp.where(row_ids == slots, 1.0, 0.0).astype(BF16)
        return c

    lax.fori_loop(0, blocks // 2, pick, 0, unroll=2)

    if half > bins:
        part_out[...] = jnp.zeros_like(part_out)

    def cross_chunk(part):
        def whiten(src):
            re = spec_in[part, src, :chunk].astype(F32)
            im = spec_in[part, src, chunk:].astype(F32)
            level = water_in[src][0:1] * (0.1 / F) + 1e-6
            factor = lax.rsqrt(re * re + im * im + level)
            return re * factor, im * factor

        def whiten_two(q, c):
            cols = pl.ds(pl.multiple_of(q * 128, 128), 128)
            one, two = whiten(2 * q), whiten(2 * q + 1)
            for k in range(2):
                first = jnp.where(lane < 64, one[k], swap(two[k]))
                second = jnp.where(lane < 64, swap(one[k]), two[k])
                at = k * chunk
                white[at:at + chunk, cols] = first.astype(BF16)
                at += 2 * chunk
                white[at:at + chunk, cols] = second.astype(BF16)
            return c

        lax.fori_loop(0, blocks // 2, whiten_two, 0, unroll=2)

        def cross(g, c):
            got = jnp.dot(white[...], onehot[g], preferred_element_type=F32)
            real = imag = None
            for w in range(2):
                at = 2 * w * chunk
                lr, rr = got[at:at + chunk, :128], got[at:at + chunk, 128:]
                at += chunk
                li, ri = got[at:at + chunk, :128], got[at:at + chunk, 128:]
                re, im = lr * rr + li * ri, li * rr - lr * ri
                real = re if real is None else real + re
                imag = im if imag is None else imag + im
            for t in range(tm):
                rows = slice(t * bins, (t + 1) * bins)
                part_out[part, t, g, :bins] = real[rows].astype(BF16)
                part_out[part, t, g, half:half + bins] = imag[rows].astype(BF16)
            return c

        lax.fori_loop(0, blocks // 2, cross, 0, unroll=4)
        each(1, tm, lambda s: part_copy(part, s).start())
        part_in[part, mine] = part_out[part, mine]

    def pack_chunk(part):
        each(1, tm, lambda s: part_copy(part, s).wait())

        def pack(g, c):
            total = part_in[part, 0, g].astype(F32)
            for t in range(1, tm):
                total += part_in[part, t, g].astype(F32)
            top, bottom = total[:half], total[half:]
            pack_out[part, 2 * g] = jnp.where(lane < 64, top, swap(bottom)).astype(BF16)
            pack_out[part, 2 * g + 1] = jnp.where(lane < 64, swap(top), bottom).astype(BF16)
            return c

        lax.fori_loop(0, blocks // 2, pack, 0, unroll=4)
        each(1, blocks, lambda s: pack_copy(part, s).start())
        pack_in[part, mine, me] = pack_out[part, me]

    def share_chunk(part):
        each(1, blocks, lambda s: pack_copy(part, s).wait())
        each(1, tm, lambda s: last_copy(part, s).start())

    def lag_chunk(part):
        each(1, tm, lambda s: last_copy(part, s).wait())
        count = tm * blocks * half
        at = slice(part * count, (part + 1) * count)
        stacked = pack_in[part].reshape(count, 128).astype(F32)
        turned = stacked * turn[0, at, :] + swap(stacked) * turn[1, at, :]
        values = jnp.concatenate([turned, swap(turned)], axis=0).astype(BF16)
        product = jnp.dot(lag[part], values, preferred_element_type=F32)
        total_out[...] = product if part == 0 else total_out[...] + product

    lag_copy.start()
    turn_copy.start()
    for part in range(2, chunks):
        for s in order:
            spec_copy(part - 2, s).wait_send()
            spec_copy(part, s).start()
    each(1, blocks, lambda s: water_copy(s).wait_recv())
    for part in range(chunks):
        each(1, blocks, lambda s: spec_copy(part, s).wait_recv())
        cross_chunk(part)
        if 0 < part < chunks - 1:
            share_chunk(part - 1)
        pack_chunk(part)
    lag_copy.wait()
    turn_copy.wait()
    if chunks > 1:
        share_chunk(chunks - 2)
    for part in range(chunks - 2):
        lag_chunk(part)
    share_chunk(chunks - 1)
    for part in range(max(0, chunks - 2), chunks):
        lag_chunk(part)
    for part in range(max(0, chunks - 2), chunks):
        for s in order:
            spec_copy(part, s).wait_send()
    each(1, blocks, lambda s: water_copy(s).wait_send())
    out[...] = total_out[...].T[:64]


def on_device(traces, station_slot, pair_stations):
    held, stations_each, length = traces.shape
    stations = station_slot.shape[0]
    blocks, tm = lax.axis_size("pairs"), lax.axis_size("tm")
    pairs_each = pair_stations.shape[0]
    assert held * stations_each == 128 and held == 2 and pairs_each == 64 and blocks % RADIX == 0
    bins_each, chunks, bins, half = split(blocks, tm)
    short = length // RADIX
    values = tm * blocks * half
    lag_rows = 2 * LAG // tm
    forward, lag, turn = tables(length, blocks, tm)
    times = (np.arange(length, dtype=np.float64) + 0.5) * (2.0 * np.pi / length)
    hann = (0.5 - 0.5 * np.cos(times)).astype(np.float32).reshape(RADIX, short)
    scale = 1.0 / math.sqrt(F * held * tm)
    vmem = pl.BlockSpec(memory_space=pltpu.VMEM)
    anywhere = pl.BlockSpec(memory_space=pl.ANY)
    dma = pltpu.SemaphoreType.DMA
    result = pl.pallas_call(
        functools.partial(kernel, blocks, tm),
        out_shape=jax.ShapeDtypeStruct((pairs_each, lag_rows), F32),
        in_specs=[anywhere, anywhere, anywhere, anywhere, anywhere, anywhere, anywhere],
        out_specs=vmem,
        scratch_shapes=[
            pltpu.VMEM((128, length), F32),
            pltpu.VMEM((128, 128), F32),
            pltpu.VMEM((RADIX, short), F32),
            pltpu.VMEM((1, stations), jnp.int32),
            pltpu.VMEM((2, pairs_each), jnp.int32),
            pltpu.VMEM((blocks, 2 * bins_each, short), BF16),
            pltpu.VMEM((chunks, lag_rows, 2 * values), BF16),
            pltpu.VMEM((stations, 128), F32),
            pltpu.VMEM((8, 128), F32),
            pltpu.VMEM((RADIX, 256, short), BF16),
            pltpu.VMEM((8, 128), F32),
            pltpu.VMEM((chunks, blocks, 2 * bins_each // chunks, 128), BF16),
            pltpu.VMEM((chunks, blocks, 2 * bins_each // chunks, 128), BF16),
            pltpu.VMEM((blocks, 8, 128), F32),
            pltpu.VMEM((blocks, 8, 128), F32),
            pltpu.VMEM((blocks // 2, stations, 256), BF16),
            pltpu.VMEM((4 * bins_each // chunks, stations), BF16),
            pltpu.VMEM((chunks, tm, blocks // 2, 2 * half, 128), BF16),
            pltpu.VMEM((chunks, tm, blocks // 2, 2 * half, 128), BF16),
            pltpu.VMEM((chunks, blocks, half, 128), BF16),
            pltpu.VMEM((chunks, tm, blocks, half, 128), BF16),
            pltpu.VMEM((2, chunks * values, 128), F32),
            pltpu.VMEM((lag_rows, 128), F32),
            dma((5,)), dma((8,)), dma((blocks,)),
            dma((blocks,)), dma((blocks,)),
            dma((chunks, blocks)), dma((chunks, blocks)),
            dma((blocks,)), dma((blocks,)),
            dma((chunks, tm)), dma((chunks, tm)),
            dma((chunks, blocks)), dma((chunks, blocks)),
            dma((chunks, tm)), dma((chunks, tm)),
        ],
        compiler_params=pltpu.CompilerParams(
            collective_id=0, has_side_effects=True, vmem_limit_bytes=56 * 1024 * 1024
        ),
    )(
        traces.reshape(128, length), jnp.asarray(hann), station_slot.reshape(1, stations),
        pair_stations.T, jnp.asarray(forward), jnp.asarray(lag), jnp.asarray(turn),
    )
    return result.T * scale


def solution(mesh):
    in_specs = (P("tm", "pairs", None), P(), P("pairs", None))
    out_specs = P("tm", "pairs")
    return jax.shard_map(
        on_device, mesh=mesh, in_specs=in_specs, out_specs=out_specs, check_vma=False
    )
```
